128 devices in a mesh: tile: 16 (over x, y), lat: 8 (over z, core).
Axes of the slice: x: 4, y: 4, z: 4, core: 2. Of those that a mesh axis runs over, the one named last changes fastest.
Arguments:
- source: bfloat16 [896, 8, 4096], P(('tile', 'lat')), may hold values from -6 to 6
- row_map: bfloat16 [40, 16, 4, 32, 64], P('lat', 'tile'), may hold values from -0.375 to 0.375
- col_map: bfloat16 [40, 4, 64, 2560], P('lat', None, None, 'tile'), may hold values from -0.75 to 0.75
- pattern: int32 [40, 16, 4], P('lat', 'tile'), may hold values from 0 to 11, as said below
- codes: int32 [40, 16, 4], P('lat', 'tile'), may hold values from 0 to 3
- need_list: int32 [16, 8, 12], P('tile'), may hold values from 0 to 895, as said below
- owner: int32 [896], replicated, may hold values from 0 to 895, as said below
Outputs:
- spectrum: float32 [640, 16, 1281], P(('tile', 'lat'))
The draws below stay inside these ranges and needn't reach their ends.
Inputs may be any that keep to these rules, and one draw needn't show every extreme that they name: need_list[t, l] names 12 distinct blocks, all held by devices of tile column t; each device that holds any of them holds exactly 3 of them. `owner`: a permutation of the slots. `pattern`: on each device every one of the 12 indices is used by some term.
All inputs are finite; a program needn't handle non-finite values.
Results may differ from the reference program's by a relative error of at most 0.0029.
Values may be sent and summed in bfloat16 or wider, within the bound.
No kernel may reach another device: no remote copies, remote signals or barrier semaphores. Data moves between devices by JAX's collectives and lax.ppermute only.
A program may use at most 64 MiB of HBM per device.

```python
import math
import jax
import jax.numpy as jnp
from jax import lax

NLON = 2560
NLAT = 1280
M = 1280
BS = 64
RB = 32
K = 4
NEED = 12
MOST = 3
SLOTS_DEV = 7
LEV = 8
BLOCKS = 896
N_TILE = 16
N_LAT = 8


def plan_tables(key):
    base = jax.random.fold_in(key, 7301)
    owner = jax.random.permutation(jax.random.fold_in(base, 1), SLOTS_DEV * N_TILE * N_LAT).astype(jnp.int32)
    holders = jnp.argsort(owner, stable=True).astype(jnp.int32)
    groups = NEED // MOST

    def one_device(index):
        device_key = jax.random.fold_in(jax.random.fold_in(base, 2), index)
        column = index // N_LAT
        sources = jax.random.permutation(jax.random.fold_in(device_key, 1), N_LAT)[:groups]

        def one_source(number, holder_lat):
            chosen = jax.random.permutation(jax.random.fold_in(device_key, 10 + number), SLOTS_DEV)[:MOST]
            return (column * N_LAT + holder_lat) * SLOTS_DEV + chosen
        slots = jax.vmap(one_source)(jnp.arange(groups, dtype=jnp.int32), sources).reshape(NEED)
        slots = jax.random.permutation(jax.random.fold_in(device_key, 3), slots)
        return holders[slots]
    needs = jax.vmap(one_device)(jnp.arange(N_TILE * N_LAT, dtype=jnp.int32))
    return (owner, needs.reshape(N_TILE, N_LAT, NEED).astype(jnp.int32))


def draw_owner(key, part):
    return plan_tables(key)[0]


def draw_need_list(key, part):
    return plan_tables(key)[1]


def draw_pattern(key, part):
    base = jax.random.fold_in(key, 5113)
    band = NLAT // (RB * N_LAT)
    total = band * K

    def one_device(index):
        device_key = jax.random.fold_in(base, index)
        head = jax.random.permutation(jax.random.fold_in(device_key, 1), NEED)
        extra = jax.random.randint(jax.random.fold_in(device_key, 2), (total,), 0, NEED)
        values = jnp.concatenate([head, extra[NEED:]])
        values = jax.random.permutation(jax.random.fold_in(device_key, 3), values)
        return values.reshape(band, K)
    table = jax.vmap(one_device)(jnp.arange(N_LAT * N_TILE, dtype=jnp.int32))
    table = table.reshape(N_LAT, N_TILE, band, K)
    return jnp.transpose(table, (0, 2, 1, 3)).reshape(NLAT // RB, N_TILE, K).astype(jnp.int32)


def place_ends(drawn, rng, smallest, largest):
    extent = drawn.shape
    index_at = [jax.random.randint(jax.random.fold_in(rng, axis), (), 0, extent[axis]) for axis in range(len(extent))]
    drawn = drawn.at[tuple(index_at)].set(smallest)
    longest = extent.index(max(extent))
    index_at[longest] = (index_at[longest] + 1) % extent[longest]
    return drawn.at[tuple(index_at)].set(largest)


def levels(rng, extent, shards, smallest, high):
    loudness = 1.0
    for axis_at, shards_of in shards:
        steps = jax.random.uniform(jax.random.fold_in(jax.random.fold_in(rng, 6), axis_at), (shards_of,), jnp.float32, smallest / len(shards), high / len(shards))
        loudness = loudness * jnp.repeat(jnp.exp(steps), extent[axis_at] // shards_of).reshape((-1,) + (1,) * (len(extent) - 1 - axis_at))
    return loudness


def normal_values(rng, shape, spread, most, shards=(), kind=jnp.bfloat16):
    entries = spread * jax.random.normal(rng, shape, jnp.float32)
    if shards:
        entries = entries * levels(rng, shape, shards, -0.22, 0.18)
    return jnp.clip(entries, -most, most).astype(kind)


def setup_inputs(seed: int = 0) -> dict:
    arg_keys = jax.random.split(jax.random.key(seed), 8)
    source = normal_values(arg_keys[0], (BLOCKS, LEV, BS * BS), 1.0, 6.0, ((0, 128),))
    row_map = normal_values(arg_keys[1], (NLAT // RB, N_TILE, K, RB, BS), (K * BS) ** -0.5, 0.375, ((0, 8), (1, 16)))
    col_map = normal_values(arg_keys[2], (NLAT // RB, K, BS, NLON), BS ** -0.5, 0.75, ((0, 8), (3, 16)))
    pattern = draw_pattern(jax.random.fold_in(arg_keys[7], 71), 0)
    codes = place_ends(jax.random.randint(arg_keys[4], (NLAT // RB, N_TILE, K), 0, 4), jax.random.fold_in(arg_keys[4], 1), 0, 3).astype(jnp.int32)
    need_list = draw_need_list(jax.random.fold_in(arg_keys[7], 71), 0)
    owner = draw_owner(jax.random.fold_in(arg_keys[7], 71), 0)
    return dict(source=source, row_map=row_map, col_map=col_map, pattern=pattern, codes=codes, need_list=need_list, owner=owner)


highest = lax.Precision.HIGHEST

def sectoral_logs():
    steps = jnp.arange(1, M, dtype=jnp.int32).astype(jnp.float32)
    terms = 0.5 * jnp.log1p(0.5 / steps)
    return jnp.concatenate([jnp.zeros((1,), jnp.float32), jnp.cumsum(terms)]) + 0.5 * math.log(0.5)

def legendre_sums(fields, pair_ids, colat, weights):
    count = pair_ids.shape[0]
    lats = colat.shape[0]
    norm_logs = sectoral_logs()
    orders = jnp.arange(M, dtype=jnp.int32)
    low_order = pair_ids
    high_order = M - 1 - pair_ids
    low_length = M - pair_ids
    cosine = jnp.cos(colat)
    log_sine = jnp.log(jnp.sin(colat))

    def sectoral(order):
        picked = lax.optimization_barrier(jnp.sum(jnp.where(order[:, None] == orders[None, :], norm_logs[None, :], 0.0), axis=1))
        exponent = picked[:, None] + order.astype(jnp.float32)[:, None] * log_sine[None, :]
        ramp = jnp.clip((exponent + 75.0) / 10.0, 0.0, 1.0)
        return jnp.exp(jnp.maximum(exponent, -75.0)) * ramp
    start_low = sectoral(low_order)
    start_high = sectoral(high_order)
    scaled = fields * weights[None, None, :, None]

    def advance(state, slot):
        previous, before = state
        is_low = slot < low_length
        order = jnp.where(is_low, low_order, high_order)
        degree = jnp.where(is_low, low_order + slot, high_order + slot - low_length)
        fresh = degree == order
        order_f = order.astype(jnp.float32)
        degree_f = degree.astype(jnp.float32)
        lower_f = degree_f - 1.0
        grows = degree > order
        ratio = jnp.where(grows, (4.0 * degree_f * degree_f - 1.0) / jnp.where(grows, degree_f * degree_f - order_f * order_f, 1.0), 0.0)
        back = degree - 1 > order
        inverse = jnp.where(back, (lower_f * lower_f - order_f * order_f) / jnp.where(back, 4.0 * lower_f * lower_f - 1.0, 1.0), 0.0)
        grown = jnp.sqrt(ratio)[:, None] * (cosine[None, :] * previous - jnp.sqrt(inverse)[:, None] * before)
        start = jnp.where(is_low[:, None], start_low, start_high)
        value = jnp.where(fresh[:, None], start, grown)
        return ((value, jnp.where(fresh[:, None], 0.0, previous)), value)

    def one_block(state, base):
        slots = base + jnp.arange(128, dtype=jnp.int32)
        state, table = lax.scan(advance, state, slots, unroll=8)
        low_mask = (slots[:, None] < low_length[None, :]).astype(jnp.float32)
        both = jnp.stack([table * low_mask[:, :, None], table * (1.0 - low_mask)[:, :, None]], axis=2)
        sums = jnp.einsum('sqhl,qhlc->qcs', both, scaled, precision=highest)
        return (state, sums)
    zeros = jnp.zeros((count, lats), jnp.float32)
    total = -(-(M + 1) // 128)
    bases = jnp.arange(total, dtype=jnp.int32) * 128
    _, sums = lax.scan(one_block, (zeros, zeros), bases)
    sums = jnp.transpose(sums, (1, 2, 0, 3)).reshape(count, fields.shape[3], total * 128)
    return sums[:, :, :M + 1]

def row_products(picked, code, rmap, cmap):
    side = rmap.shape[2]
    blocks = picked.reshape(picked.shape[0], picked.shape[1], side, side)
    turned = jnp.swapaxes(blocks, 2, 3)
    chosen = jnp.where((code % 2 == 1)[:, None, None, None], turned, blocks)
    row_flip = (code == 1) | (code == 2)
    col_flip = (code == 2) | (code == 3)
    rmap = jnp.where(row_flip[:, None, None], rmap[:, :, ::-1], rmap)
    cmap = jnp.where(col_flip[:, None, None], cmap[:, ::-1, :], cmap)
    inner = jnp.einsum('klrc,kcx->klrx', chosen.astype(jnp.float32), cmap.astype(jnp.float32), precision=highest)
    inner = lax.optimization_barrier(inner.astype(jnp.bfloat16)).astype(jnp.float32)
    return jnp.einsum('kar,klrx->lax', rmap.astype(jnp.float32), inner, precision=highest)

def reference(source, row_map, col_map, pattern, codes, need_list, owner):
    band = NLAT // (RB * N_LAT)
    width = NLON // N_TILE

    def one_row(row):
        needs = lax.dynamic_index_in_dim(need_list, (row // band).astype(jnp.int32), 1, keepdims=False)
        ids = jnp.take_along_axis(needs, pattern[row], axis=1)
        slots = jnp.take(owner, ids)
        picked = jnp.take(source, slots.reshape(-1), axis=0).reshape((N_TILE, K) + source.shape[1:])
        cmap = jnp.transpose(col_map[row].reshape(K, BS, N_TILE, width), (2, 0, 1, 3))
        rows = jax.vmap(row_products)(picked, codes[row], row_map[row], cmap)
        return jnp.transpose(rows, (1, 2, 0, 3)).reshape(LEV, RB, NLON)
    rows = lax.map(one_row, jnp.arange(NLAT // RB, dtype=jnp.int32))
    field = jnp.transpose(rows, (1, 0, 2, 3)).reshape(LEV, NLAT, NLON)
    spectral = jnp.fft.rfft(field, axis=2)[:, :, :M] / math.sqrt(NLON)
    parts = jnp.stack([jnp.real(spectral), jnp.imag(spectral)]).astype(jnp.float32)
    combined = jnp.transpose(parts, (3, 2, 0, 1)).reshape(M, NLAT, 2 * LEV)
    latitude = jnp.arange(NLAT, dtype=jnp.int32).astype(jnp.float32)
    colat = math.pi * (latitude + 0.75) / (NLAT + 0.5)
    weights = math.pi * jnp.sin(colat) * math.sqrt(NLAT) / (NLAT + 0.5)

    def one_group(group):
        pair_ids = group * 64 + jnp.arange(64, dtype=jnp.int32)
        low = lax.dynamic_slice_in_dim(combined, group * 64, 64, 0)
        high = lax.dynamic_slice_in_dim(combined, M - (group + 1) * 64, 64, 0)[::-1]
        fields = jnp.stack([low, high], axis=1)
        return legendre_sums(fields, pair_ids, colat, weights)
    result = lax.map(one_group, jnp.arange(M // 128, dtype=jnp.int32))
    return result.reshape(M // 2, 2 * LEV, M + 1)
```

```python
import math

import jax
import jax.numpy as jnp
import numpy as np
from jax import lax
from jax.experimental import pallas as pl
from jax.experimental.pallas import tpu as pltpu
from jax.sharding import PartitionSpec as P

NLON = 2560
NLAT = 1280
M = 1280
NEED = 12
MOST = 3
LEV = 8
PAIRS = 5
STEPS = 1296
CHUNK = 144
MIB = 2**20
F32 = jnp.float32
BF16 = jnp.bfloat16

EVENS = [(i, h, c) for i in range(5) for h in range(2) if (i + h) % 2 == 0 for c in range(2)]
ODDS = [(i, h, c) for i in range(5) for h in range(2) if (i + h) % 2 == 1 for c in range(2)]
SLOT = {e: 2 * w for w, e in enumerate(EVENS)} | {e: 2 * w + 1 for w, e in enumerate(ODDS)}


def dft_tables():
    s = np.arange(8)
    points = np.concatenate(
        [(s[:, None] * 160 + np.arange(128)).ravel(), (s[:, None] * 160 + np.arange(128, 160)).ravel()]
    )
    l2, t = np.meshgrid(np.arange(4), np.arange(16), indexing="ij")
    order = np.zeros((2, 10, 2, 64), np.int64)
    part = np.zeros((2, 10, 2, 64), np.int64)
    for q in range(2):
        for w in range(10):
            for half in range(2):
                i, h, c = (EVENS if q == half else ODDS)[w]
                pair = 5 * (t * 8 + 2 * l2 + half) + i
                order[q, w, half] = (pair if h == 0 else M - 1 - pair).ravel()
                part[q, w, half] = c
    order, part = order.reshape(2, 1, 1280), part.reshape(2, 1, 1280)
    angle = (points[None, :, None] * order % NLON) * (2.0 * np.pi / NLON)
    table = np.where(part == 0, np.cos(angle), -np.sin(angle)) / math.sqrt(NLON)
    high = table.astype(BF16)
    low = (table - high.astype(np.float64)).astype(BF16)
    return high, low


def latitudes():
    b, a2, l, t = np.meshgrid(np.arange(5), np.arange(2), np.arange(4), np.arange(16), indexing="ij")
    lat = (l * 160 + b * 32 + 2 * t + a2).reshape(5, 128)
    colat = np.pi * (lat + 0.75) / (NLAT + 0.5)
    return np.concatenate([colat, np.full((3, 128), np.pi / 2)])


def holder_of(owner_ref, need_ref, at):
    holder = owner_ref[need_ref[at]]
    device = (holder * 9363) >> 16
    return device & 7, holder - 7 * device


def pack_kernel(owner_ref, need_ref, me_ref, source_ref, out_ref, rows_ref, turned_ref):
    lane = lax.broadcasted_iota(jnp.int32, (32, 128), 1)
    for s in range(7):
        for i in range(32):
            rows_ref[pl.ds(i, 8, stride=32), :] = source_ref[s, :, i * 128 : (i + 1) * 128].astype(F32)
        for lp in range(4):
            one = rows_ref[lp * 64 : lp * 64 + 32, :]
            two = rows_ref[lp * 64 + 32 : lp * 64 + 64, :]
            top = jnp.where(lane < 64, one, pltpu.roll(two, 64, 1))
            low = jnp.where(lane < 64, pltpu.roll(one, 64, 1), two)
            at = slice(lp * 128, (lp + 1) * 128)
            turned_ref[s, 0:32, at] = top.astype(BF16)
            turned_ref[s, 32:64, at] = low.astype(BF16)
    me = me_ref[0]

    def one_dest(dest, _):
        def one_need(i, count):
            lat, slot = holder_of(owner_ref, need_ref, dest * NEED + i)

            @pl.when(lat == me)
            def _():
                out_ref[dest * MOST + jnp.minimum(count, MOST - 1)] = turned_ref[slot]

            return count + (lat == me).astype(jnp.int32)

        lax.fori_loop(0, NEED, one_need, jnp.int32(0))
        return 0

    lax.fori_loop(0, 8, one_dest, 0)


def regrid_kernel(
    owner_ref, need_ref, me_ref, pattern_ref, codes_ref, blocks_ref, cols_ref, rmat_ref, out_ref,
    left_ref, acc_ref, tail_ref, packed_ref, where_ref, seen_ref,
):
    me = me_ref[0]
    for l in range(8):
        seen_ref[l] = 0

    def locate(i, _):
        lat, _ = holder_of(owner_ref, need_ref, me * NEED + i)
        rank = seen_ref[lat]
        where_ref[i] = lat * MOST + jnp.minimum(rank, MOST - 1)
        seen_ref[lat] = rank + 1
        return 0

    lax.fori_loop(0, NEED, locate, 0)
    tail_ref[...] = jnp.zeros_like(tail_ref)
    lane = lax.broadcasted_iota(jnp.int32, (64, 128), 1)
    zero = jnp.zeros((64, 128), BF16)
    south = me >= 4

    for b in range(5):
        row_block = jnp.where(south, 4 - b, b)
        sums = [None, None]
        for k in range(4):
            term = row_block * 4 + k
            at = where_ref[pattern_ref[term]]
            odd = codes_ref[term] & 1

            @pl.when(odd == 0)
            def _():
                for lp in range(4):
                    tile = blocks_ref[at, :, lp * 128 : (lp + 1) * 128]
                    left_ref[lp * 128 : lp * 128 + 64, :] = jnp.where(lane < 64, tile, zero)
                    left_ref[lp * 128 + 64 : lp * 128 + 128, :] = jnp.where(lane < 64, zero, tile)

            @pl.when(odd == 1)
            def _():
                for lp in range(4):
                    tile = blocks_ref[at, :, lp * 128 : (lp + 1) * 128].astype(F32)
                    both = jnp.concatenate([tile, jnp.zeros((64, 128), F32)], axis=0)
                    left_ref[lp * 128 : (lp + 1) * 128, :] = both.T.astype(BF16)

            inner = jnp.dot(left_ref[...], cols_ref[term], preferred_element_type=F32).astype(BF16)
            for half in range(2):
                new = jnp.dot(
                    rmat_ref[term], inner[half * 256 : (half + 1) * 256], preferred_element_type=F32
                )
                sums[half] = new if k == 0 else sums[half] + new
        for half in range(2):
            acc_ref[half * 128 : (half + 1) * 128, :] = sums[half][:, :128]
            tail_ref[half * 128 : (half + 1) * 128, 0:32] = sums[half][:, 128:160]
        for t in range(16):
            main = [acc_ref[pl.ds(2 * t + a, 8, stride=32), :] for a in range(2)]
            out_ref[t, b * 16 : (b + 1) * 16, :] = jnp.concatenate(main, axis=0).astype(BF16)
            rest = jnp.concatenate([tail_ref[pl.ds(2 * t + a, 8, stride=32), :] for a in range(2)], axis=0)
            if b == 0:
                packed_ref[0, t] = rest
            elif b < 4:
                packed_ref[0, t] += pltpu.roll(rest, 32 * b, 1)
            else:
                packed_ref[1, t] = rest
    for t in range(16):
        out_ref[t, 80:96, :] = packed_ref[0, t].astype(BF16)
        out_ref[t, 96:112, :] = packed_ref[1, t].astype(BF16)


def dft_kernel(rows_ref, high_ref, low_ref, out_ref, both_ref, sums_ref, spread_ref):
    step = pl.program_id(0)
    lane = lax.broadcasted_iota(jnp.int32, (80, 128), 1)

    @pl.when(step == 0)
    def _():
        quarter = lax.broadcasted_iota(jnp.int32, (16, 128), 1) // 32
        sums_ref[1600:1664, :] = jnp.zeros((64, 128), F32)
        for q in range(2):

            def mixed(s, at):
                one, two = rows_ref[s, at, :].astype(F32), rows_ref[s + 8, at, :].astype(F32)
                return one + two if q == 0 else one - two

            def put(row, count, at, value):
                high = value.astype(BF16)
                both_ref[q, row : row + count, at] = high
                both_ref[q, 80 + row : 80 + row + count, at] = (value - high.astype(F32)).astype(BF16)

            for s in range(8):
                put(0, 80, slice(s * 128, (s + 1) * 128), mixed(s, slice(0, 80)))
            for group in range(2):
                first = [mixed(group * 4 + j, slice(80, 96)) for j in range(4)]
                last = [mixed(group * 4 + j, slice(96, 112)) for j in range(4)]
                for b in range(5):
                    value = jnp.zeros((16, 128), F32)
                    for j in range(4):
                        tile = first[j] if b < 4 else last[j]
                        shift = (32 * (j - (b if b < 4 else 0))) % 128
                        moved = tile if shift == 0 else pltpu.roll(tile, shift, 1)
                        value = jnp.where(quarter == j, moved, value)
                    put(b * 16, 16, slice(1024 + group * 128, 1152 + group * 128), value)

    outs = []
    for q in range(2):
        main = jnp.dot(both_ref[q], high_ref[q], preferred_element_type=F32)
        rest = jnp.dot(both_ref[q, 0:80, :], low_ref[q], preferred_element_type=F32)
        outs.append(main[0:80] + main[80:160] + rest)
    for half in range(2):
        at = slice(half * 128, (half + 1) * 128)
        even = jnp.where(lane < 64, outs[0][:, at], outs[1][:, at])
        odd = jnp.where(lane < 64, outs[1][:, at], outs[0][:, at])
        base = pl.multiple_of(step * 320 + half * 160, 16)
        sums_ref[pl.ds(base, 80), :] = even
        sums_ref[pl.ds(base + 80, 80), :] = odd

    @pl.when(step == pl.num_programs(0) - 1)
    def _():
        for k in range(13):
            turned = sums_ref[k * 128 : (k + 1) * 128, :].T
            for group in range(8):
                l = 2 * (group % 4) + group // 4
                spread_ref[pl.ds(l * 256 + k, 16, stride=16), :] = turned[group * 16 : (group + 1) * 16]
        for d in range(128):
            out_ref[d] = spread_ref[d * 16 : (d + 1) * 16, :].astype(BF16)


def table_kernel(coef_ref, switch_ref, cosine_ref, low_ref, start_ref, high_out, low_out, state_ref, rows_ref):
    step = pl.program_id(0)

    @pl.when(step == 0)
    def _():
        state_ref[...] = jnp.zeros_like(state_ref)

    cosine = cosine_ref[...]
    switches = [switch_ref[i] for i in range(PAIRS)]

    def sixteen(part, state):
        base = step * CHUNK + part * 16
        state = list(state)
        for k in range(16):
            slot = base + k
            for i in range(PAIRS):
                one, two = state[2 * i], state[2 * i + 1]
                grow = coef_ref[(2 * i) * STEPS + slot]
                back = coef_ref[(2 * i + 1) * STEPS + slot]
                value = (cosine * grow) * one - two * back
                if k == 0:
                    value = jnp.where(slot == 0, low_ref[i], value)
                value = jnp.where(slot == switches[i], start_ref[i], value)
                state[2 * i], state[2 * i + 1] = value, one
                rows_ref[i, k * 8 : (k + 1) * 8, :] = value
        at = pl.ds(pl.multiple_of(part * 16, 16), 16)
        for i in range(PAIRS):
            for b in range(5):
                value = rows_ref[i, pl.ds(b, 16, stride=8), :]
                high = value.astype(BF16)
                high_out[i, at, b * 128 : (b + 1) * 128] = high
                low_out[i, at, b * 128 : (b + 1) * 128] = (value - high.astype(F32)).astype(BF16)
        return tuple(state)

    state = lax.fori_loop(0, CHUNK // 16, sixteen, tuple(state_ref[j] for j in range(2 * PAIRS)))
    for j in range(2 * PAIRS):
        state_ref[j] = state[j]


def sums_kernel(first_ref, blocks_ref, high_ref, low_ref, out_ref, spread_ref, turned_ref, left_ref):
    step = pl.program_id(0)

    @pl.when(step == 0)
    def _():
        lane = lax.broadcasted_iota(jnp.int32, (8, 128), 1)
        for d in range(128):
            spread_ref[d * 16 : (d + 1) * 16, :] = blocks_ref[d].astype(F32)
        for k in range(13):
            parts = [spread_ref[pl.ds(l * 256 + k, 16, stride=16), :] for l in (0, 1, 2, 3, 7, 6, 5, 4)]
            turned_ref[k * 128 : (k + 1) * 128, :] = jnp.concatenate(parts, axis=0).T
        for i in range(PAIRS):
            for h in range(2):
                for b in range(5):
                    north, south = [], []
                    for c in range(2):
                        base = SLOT[(i, h, c)] * 80 + b * 16
                        one, two = turned_ref[base : base + 8, :], turned_ref[base + 8 : base + 16, :]
                        north.append(jnp.where(lane < 64, one, pltpu.roll(two, 64, 1)))
                        south.append(jnp.where(lane < 64, pltpu.roll(one, 64, 1), two))
                    at = slice(b * 128, (b + 1) * 128)
                    left_ref[i, h * 16 : h * 16 + 16, at] = jnp.concatenate(north, axis=0).astype(BF16)
                    left_ref[i, 32 + h * 16 : 48 + h * 16, at] = jnp.concatenate(south, axis=0).astype(BF16)

    left = left_ref[step]
    both_last = (((1,), (1,)), ((), ()))
    sums = lax.dot_general(left, high_ref[0], both_last, preferred_element_type=F32)
    sums += lax.dot_general(left, low_ref[0], both_last, preferred_element_type=F32)
    pair = first_ref[0] + step
    slot = lax.broadcasted_iota(jnp.int32, (16, STEPS), 1)
    low = sums[0:16] + jnp.where(slot & 1 == 0, sums[32:48], -sums[32:48])
    high = sums[16:32] + jnp.where((slot + pair) & 1 == 0, sums[48:64], -sums[48:64])
    result = jnp.where(slot < M - pair, low, high)
    out_ref[0] = result[:, : M + 1]


def vmem(shape=None, index=None):
    if shape is None:
        return pl.BlockSpec(memory_space=pltpu.VMEM)
    return pl.BlockSpec(shape, index)


SMEM = pl.BlockSpec(memory_space=pltpu.SMEM)


def params(limit):
    return pltpu.CompilerParams(vmem_limit_bytes=limit * MIB)


def cost(flops, moved):
    return pl.CostEstimate(flops=flops, bytes_accessed=moved, transcendentals=0)


def legendre_table(first):
    pair = first + jnp.arange(PAIRS, dtype=jnp.int32)
    slot = jnp.arange(STEPS, dtype=jnp.int32)[None, :]
    is_low = slot < (M - pair)[:, None]
    order = jnp.where(is_low, pair[:, None], M - 1 - pair[:, None])
    degree = jnp.where(is_low, pair[:, None] + slot, slot - 1)
    live = slot <= M
    grows = (degree > order) & live
    back = (degree - 1 > order) & live
    order_f, degree_f = order.astype(F32), degree.astype(F32)
    lower_f = degree_f - 1.0
    ratio = (4.0 * degree_f * degree_f - 1.0) / jnp.where(grows, degree_f * degree_f - order_f * order_f, 1.0)
    inverse = (lower_f * lower_f - order_f * order_f) / jnp.where(back, 4.0 * lower_f * lower_f - 1.0, 1.0)
    grow = jnp.where(grows, jnp.sqrt(jnp.where(grows, ratio, 1.0)), 0.0)
    keep = jnp.where(back, grow * jnp.sqrt(jnp.where(back, inverse, 1.0)), 0.0)
    coef = jnp.stack([grow, keep], axis=1).reshape(-1)

    terms = 0.5 * np.log1p(0.5 / np.arange(1, M, dtype=np.float64))
    logs = np.concatenate([np.zeros(1), np.cumsum(terms)]) + 0.5 * math.log(0.5)
    logs = jnp.asarray(logs.astype(np.float32))
    colat = latitudes()
    log_sine = jnp.asarray(np.log(np.sin(colat)).astype(np.float32))
    cosine = jnp.asarray(np.cos(colat).astype(np.float32))
    weight = jnp.asarray((np.pi * np.sin(colat) * math.sqrt(NLAT) / (NLAT + 0.5)).astype(np.float32))
    low_logs = lax.dynamic_slice(logs, (first,), (PAIRS,))
    high_logs = lax.dynamic_slice(logs, (M - PAIRS - first,), (PAIRS,))[::-1]

    def sectoral(picked, which):
        exponent = picked[:, None, None] + which.astype(F32)[:, None, None] * log_sine[None]
        ramp = jnp.clip((exponent + 75.0) / 10.0, 0.0, 1.0)
        return jnp.exp(jnp.maximum(exponent, -75.0)) * ramp * weight[None]

    low = sectoral(low_logs, pair)
    high = sectoral(high_logs, M - 1 - pair)
    shape = jax.ShapeDtypeStruct((PAIRS, STEPS, 640), BF16)
    block = vmem((PAIRS, CHUNK, 640), lambda g: (0, g, 0))
    return pl.pallas_call(
        table_kernel,
        grid=(STEPS // CHUNK,),
        out_shape=(shape, shape),
        in_specs=[SMEM, SMEM, vmem(), vmem(), vmem()],
        out_specs=(block, block),
        scratch_shapes=[pltpu.VMEM((2 * PAIRS, 8, 128), F32), pltpu.VMEM((PAIRS, 128, 128), F32)],
        compiler_params=params(16),
        cost_estimate=cost(60_000_000, 16_600_000),
        name="legendre_table",
    )(coef, M - pair, cosine, low, high)


def body(source, row_map, col_map, pattern, codes, need_list, owner):
    lat_me = lax.axis_index("lat").astype(jnp.int32)
    tile_me = lax.axis_index("tile").astype(jnp.int32)
    first = (tile_me * lax.axis_size("lat") + lat_me) * PAIRS
    me = lat_me.reshape(1)
    needs = need_list.reshape(-1)
    outgoing = pl.pallas_call(
        pack_kernel,
        out_shape=jax.ShapeDtypeStruct((8 * MOST, 64, 512), BF16),
        in_specs=[SMEM, SMEM, SMEM, vmem()],
        out_specs=vmem(),
        scratch_shapes=[pltpu.VMEM((256, 128), F32), pltpu.VMEM((7, 64, 512), BF16)],
        compiler_params=params(16),
        cost_estimate=cost(1_000_000, 2_000_000),
        name="pack",
    )(owner, needs, me, source)
    incoming = lax.all_to_all(outgoing, "lat", split_axis=0, concat_axis=0, tiled=True)

    high, low = legendre_table(first)

    code = codes.reshape(-1)
    odd = (code % 2 == 1)[:, None, None]
    rmap = row_map.reshape(20, 32, 64)
    rmap = jnp.where(((code == 1) | (code == 2))[:, None, None], rmap[:, :, ::-1], rmap)
    rmap = jnp.where(lat_me >= 4, rmap[:, ::-1, :], rmap)
    halves = jnp.swapaxes(rmap.reshape(20, 32, 32, 2), 2, 3).reshape(20, 32, 64)
    rmap = jnp.where(odd, rmap, halves)
    eye = jnp.eye(4, dtype=BF16)
    rmat = (eye[None, :, None, :, None] * rmap[:, None, :, None, :]).reshape(20, 128, 256)
    cmap = col_map.reshape(20, 64, 160)
    cmap = jnp.where(((code == 2) | (code == 3))[:, None, None], cmap[:, ::-1, :], cmap)
    halves = jnp.swapaxes(cmap.reshape(20, 32, 2, 160), 1, 2).reshape(20, 64, 160)
    cols = jnp.concatenate([jnp.where(odd, halves, cmap), jnp.where(odd, 0, cmap)], axis=1)

    field = pl.pallas_call(
        regrid_kernel,
        out_shape=jax.ShapeDtypeStruct((16, 112, 128), BF16),
        in_specs=[SMEM] * 5 + [vmem()] * 3,
        out_specs=vmem(),
        scratch_shapes=[
            pltpu.VMEM((512, 128), BF16),
            pltpu.VMEM((256, 128), F32),
            pltpu.VMEM((256, 128), F32),
            pltpu.VMEM((2, 16, 16, 128), F32),
            pltpu.SMEM((16,), jnp.int32),
            pltpu.SMEM((8,), jnp.int32),
        ],
        compiler_params=params(32),
        cost_estimate=cost(700_000_000, 5_000_000),
        name="regrid",
    )(owner, needs, me, pattern.reshape(-1), code, incoming, cols, rmat)
    rows = lax.all_to_all(field, "tile", split_axis=0, concat_axis=0, tiled=True)

    table_high, table_low = (jnp.asarray(t) for t in dft_tables())
    table = vmem((2, 1280, 256), lambda g: (0, 0, g))
    spectral = pl.pallas_call(
        dft_kernel,
        grid=(5,),
        out_shape=jax.ShapeDtypeStruct((128, 16, 128), BF16),
        in_specs=[vmem((16, 112, 128), lambda g: (0, 0, 0)), table, table],
        out_specs=vmem((128, 16, 128), lambda g: (0, 0, 0)),
        scratch_shapes=[
            pltpu.VMEM((2, 160, 1280), BF16),
            pltpu.VMEM((1664, 128), F32),
            pltpu.VMEM((2048, 128), F32),
        ],
        compiler_params=params(32),
        cost_estimate=cost(1_000_000_000, 14_000_000),
        name="dft",
    )(rows, table_high, table_low)
    arranged = lax.all_to_all(spectral, ("lat", "tile"), split_axis=0, concat_axis=0, tiled=True)

    part = vmem((1, STEPS, 640), lambda g: (g, 0, 0))
    return pl.pallas_call(
        sums_kernel,
        grid=(PAIRS,),
        out_shape=jax.ShapeDtypeStruct((PAIRS, 2 * LEV, M + 1), F32),
        in_specs=[SMEM, vmem((128, 16, 128), lambda g: (0, 0, 0)), part, part],
        out_specs=vmem((1, 2 * LEV, M + 1), lambda g: (g, 0, 0)),
        scratch_shapes=[
            pltpu.VMEM((2048, 128), F32),
            pltpu.VMEM((1664, 128), F32),
            pltpu.VMEM((PAIRS, 64, 640), BF16),
        ],
        compiler_params=params(32),
        cost_estimate=cost(2_000_000_000, 17_000_000),
        name="sums",
    )(first.reshape(1), arranged, high, low)


def solution(mesh):
    placed = (
        P(("tile", "lat"), None, None),
        P("lat", "tile", None, None, None),
        P("lat", None, None, "tile"),
        P("lat", "tile", None),
        P("lat", "tile", None),
        P("tile", None, None),
        P(),
    )
    return jax.shard_map(
        body, mesh=mesh, in_specs=placed, out_specs=P(("tile", "lat"), None, None), check_vma=False
    )
```

```python
import math

import jax
import jax.numpy as jnp
import numpy as np
from jax import lax
from jax.experimental import pallas as pl
from jax.experimental.pallas import tpu as pltpu
from jax.sharding import PartitionSpec as P

NLON = 2560
NLAT = 1280
M = 1280
NEED = 12
MOST = 3
LEV = 8
PAIRS = 5
STEPS = 1296
CHUNK = 144
MIB = 2**20
F32 = jnp.float32
BF16 = jnp.bfloat16

EVENS = [(i, h, c) for i in range(5) for h in range(2) if (i + h) % 2 == 0 for c in range(2)]
ODDS = [(i, h, c) for i in range(5) for h in range(2) if (i + h) % 2 == 1 for c in range(2)]
SLOT = {e: 2 * w for w, e in enumerate(EVENS)} | {e: 2 * w + 1 for w, e in enumerate(ODDS)}


def dft_tables():
    s = np.arange(8)
    points = np.concatenate(
        [(s[:, None] * 160 + np.arange(128)).ravel(), (s[:, None] * 160 + np.arange(128, 160)).ravel()]
    )
    l2, t = np.meshgrid(np.arange(4), np.arange(16), indexing="ij")
    order = np.zeros((2, 10, 2, 64), np.int64)
    part = np.zeros((2, 10, 2, 64), np.int64)
    for q in range(2):
        for w in range(10):
            for half in range(2):
                i, h, c = (EVENS if q == half else ODDS)[w]
                pair = 5 * (t * 8 + 2 * l2 + half) + i
                order[q, w, half] = (pair if h == 0 else M - 1 - pair).ravel()
                part[q, w, half] = c
    order, part = order.reshape(2, 1, 1280), part.reshape(2, 1, 1280)
    angle = (points[None, :, None] * order % NLON) * (2.0 * np.pi / NLON)
    table = np.where(part == 0, np.cos(angle), -np.sin(angle)) / math.sqrt(NLON)
    high = table.astype(BF16)
    low = (table - high.astype(np.float64)).astype(BF16)
    return [np.ascontiguousarray(x.reshape(2, 1280, 5, 256).transpose(2, 0, 1, 3)) for x in (high, low)]


def latitudes():
    b, a2, l, t = np.meshgrid(np.arange(5), np.arange(2), np.arange(4), np.arange(16), indexing="ij")
    lat = (l * 160 + b * 32 + 2 * t + a2).reshape(5, 128)
    colat = np.pi * (lat + 0.75) / (NLAT + 0.5)
    return np.concatenate([colat, np.full((3, 128), np.pi / 2)])


def holder_of(owner_ref, need_ref, dest, i):
    holder = owner_ref[need_ref[dest, i]]
    device = (holder * 9363) >> 16
    return device & 7, holder - 7 * device


def pack_kernel(owner_ref, need_ref, me_ref, source_hbm, out_ref, source_ref, rows_ref, turned_ref, list_ref, sems):
    loads = [pltpu.make_async_copy(source_hbm.at[s], source_ref.at[s], sems.at[s]) for s in range(7)]
    for load in loads:
        load.start()
    lane = lax.broadcasted_iota(jnp.int32, (32, 128), 1)
    me = me_ref[0]
    for at in range(8 * MOST):
        list_ref[at] = 0
    for dest in range(8):
        count = jnp.int32(0)
        for i in range(NEED):
            lat, slot = holder_of(owner_ref, need_ref, dest, i)
            hit = lat == me
            list_ref[jnp.where(hit, dest * MOST + jnp.minimum(count, MOST - 1), 8 * MOST)] = slot
            count = count + hit.astype(jnp.int32)
    for s in range(7):
        loads[s].wait()
        for i in range(32):
            rows_ref[s % 2, pl.ds(i, 8, stride=32), :] = source_ref[s, :, i * 128 : (i + 1) * 128].astype(F32)
        for lp in range(4):
            one = rows_ref[s % 2, lp * 64 : lp * 64 + 32, :]
            two = rows_ref[s % 2, lp * 64 + 32 : lp * 64 + 64, :]
            top = jnp.where(lane < 64, one, pltpu.roll(two, 64, 1))
            low = jnp.where(lane < 64, pltpu.roll(one, 64, 1), two)
            at = slice(lp * 128, (lp + 1) * 128)
            turned_ref[s, 0:32, at] = top.astype(BF16)
            turned_ref[s, 32:64, at] = low.astype(BF16)
    for at in range(8 * MOST):
        out_ref[at] = turned_ref[list_ref[at]]


def regrid_kernel(
    owner_ref, need_ref, me_ref, pattern_ref, codes_ref, blocks_hbm, cols_hbm, rmat_hbm, out_ref,
    blocks_ref, cols_ref, rmat_ref, sems, forms_ref, acc_ref, tail_ref, packed_ref, seen_ref,
):
    me = me_ref[0]
    maps = [
        pltpu.make_async_copy(cols_hbm, cols_ref, sems.at[NEED]),
        pltpu.make_async_copy(rmat_hbm, rmat_ref, sems.at[NEED + 1]),
    ]
    for l in range(8):
        seen_ref[l] = 0
    tail_ref[...] = jnp.zeros_like(tail_ref)
    lane = lax.broadcasted_iota(jnp.int32, (64, 128), 1)
    zero = jnp.zeros((64, 128), BF16)
    empty = jnp.zeros((64, 128), F32)
    south = me >= 4

    loads = []
    for i in range(NEED):
        lat, _ = holder_of(owner_ref, need_ref, me, i)
        rank = seen_ref[lat]
        at = lat * MOST + jnp.minimum(rank, MOST - 1)
        seen_ref[lat] = rank + 1
        loads.append(pltpu.make_async_copy(blocks_hbm.at[at], blocks_ref.at[i], sems.at[i]))
        loads[i].start()
    for move in maps:
        move.start()
    for i in range(NEED):
        loads[i].wait()
        for lp in range(4):
            tile = blocks_ref[i, :, lp * 128 : (lp + 1) * 128]
            forms_ref[2 * i, lp * 128 : lp * 128 + 64, :] = jnp.where(lane < 64, tile, zero)
            forms_ref[2 * i, lp * 128 + 64 : lp * 128 + 128, :] = jnp.where(lane < 64, zero, tile)
            both = jnp.concatenate([tile.astype(F32), empty], axis=0)
            forms_ref[2 * i + 1, lp * 128 : (lp + 1) * 128, :] = both.T.astype(BF16)

    for move in maps:
        move.wait()
    for b in range(5):
        row_block = jnp.where(south, 4 - b, b)
        sums = [None, None]
        for k in range(4):
            term = row_block * 4 + k
            form = forms_ref[pattern_ref[0, k, row_block] * 2 + (codes_ref[0, k, row_block] & 1)]
            inner = jnp.dot(form, cols_ref[term], preferred_element_type=F32).astype(BF16)
            for half in range(2):
                new = jnp.dot(
                    rmat_ref[term], inner[half * 256 : (half + 1) * 256], preferred_element_type=F32
                )
                sums[half] = new if k == 0 else sums[half] + new
        for half in range(2):
            acc_ref[b % 2, half * 128 : (half + 1) * 128, :] = sums[half][:, :128]
            tail_ref[b % 2, half * 128 : (half + 1) * 128, 0:32] = sums[half][:, 128:160]
        for t in range(16):
            at = [jnp.where(south, 31 - (2 * t + a), 2 * t + a) for a in range(2)]
            main = [acc_ref[b % 2, pl.ds(at[a], 8, stride=32), :] for a in range(2)]
            out_ref[t, b * 16 : (b + 1) * 16, :] = jnp.concatenate(main, axis=0).astype(BF16)
            rest = jnp.concatenate([tail_ref[b % 2, pl.ds(at[a], 8, stride=32), :] for a in range(2)], axis=0)
            if b == 0:
                packed_ref[t] = rest
            elif b < 4:
                packed_ref[t] += pltpu.roll(rest, 32 * b, 1)
            else:
                out_ref[t, 96:112, :] = rest.astype(BF16)
    for t in range(16):
        out_ref[t, 80:96, :] = packed_ref[t].astype(BF16)


def dft_kernel(rows_ref, high_hbm, low_hbm, out_ref, high_ref, low_ref, sems, both_ref, sums_ref, spread_ref):
    step = pl.program_id(0)
    lane = lax.broadcasted_iota(jnp.int32, (80, 128), 1)

    def load(g):
        return (
            pltpu.make_async_copy(high_hbm.at[g], high_ref.at[g], sems.at[g]),
            pltpu.make_async_copy(low_hbm.at[g], low_ref.at[g], sems.at[5 + g]),
        )

    @pl.when(step == 0)
    def _():
        for g in range(5):
            for move in load(g):
                move.start()
        quarter = lax.broadcasted_iota(jnp.int32, (16, 128), 1) // 32
        sums_ref[1600:1664, :] = jnp.zeros((64, 128), F32)
        for q in range(2):

            def mixed(s, at):
                one, two = rows_ref[s, at, :].astype(F32), rows_ref[s + 8, at, :].astype(F32)
                return one + two if q == 0 else one - two

            def put(row, count, at, value):
                high = value.astype(BF16)
                both_ref[q, row : row + count, at] = high
                both_ref[q, 80 + row : 80 + row + count, at] = (value - high.astype(F32)).astype(BF16)

            for s in range(8):
                put(0, 80, slice(s * 128, (s + 1) * 128), mixed(s, slice(0, 80)))
            for group in range(2):
                first = [mixed(group * 4 + j, slice(80, 96)) for j in range(4)]
                last = [mixed(group * 4 + j, slice(96, 112)) for j in range(4)]
                for b in range(5):
                    value = jnp.zeros((16, 128), F32)
                    for j in range(4):
                        tile = first[j] if b < 4 else last[j]
                        shift = (32 * (j - (b if b < 4 else 0))) % 128
                        moved = tile if shift == 0 else pltpu.roll(tile, shift, 1)
                        value = jnp.where(quarter == j, moved, value)
                    put(b * 16, 16, slice(1024 + group * 128, 1152 + group * 128), value)

    for move in load(step):
        move.wait()
    outs = []
    for q in range(2):
        main = jnp.dot(both_ref[q], high_ref[step, q], preferred_element_type=F32)
        rest = jnp.dot(both_ref[q, 0:80, :], low_ref[step, q], preferred_element_type=F32)
        outs.append(main[0:80] + main[80:160] + rest)
    for half in range(2):
        at = slice(half * 128, (half + 1) * 128)
        even = jnp.where(lane < 64, outs[0][:, at], outs[1][:, at])
        odd = jnp.where(lane < 64, outs[1][:, at], outs[0][:, at])
        base = pl.multiple_of(step * 320 + half * 160, 16)
        sums_ref[pl.ds(base, 80), :] = even
        sums_ref[pl.ds(base + 80, 80), :] = odd

    @pl.when(step == pl.num_programs(0) - 1)
    def _():
        for k in range(13):
            turned = sums_ref[k * 128 : (k + 1) * 128, :].T
            for group in range(8):
                l = 2 * (group % 4) + group // 4
                spread_ref[pl.ds(l * 256 + k, 16, stride=16), :] = turned[group * 16 : (group + 1) * 16]
        for d in range(128):
            out_ref[d] = spread_ref[d * 16 : (d + 1) * 16, :].astype(BF16)


def table_kernel(
    device_ref, codes_ref, logs_ref, coef_ref, colat_ref, rmap_ref, cmap_ref, rsel_ref, csel_ref,
    high_out, low_out, cols_out, rmat_out, state_ref, start_ref, rows_ref,
):
    step = pl.program_id(0)
    first = device_ref[0] * PAIRS

    @pl.when(step == 0)
    def _():
        state_ref[...] = jnp.zeros_like(state_ref)
        log_sine, weight = colat_ref[1], colat_ref[2]
        for i in range(PAIRS):
            for h in range(2):
                order = first + i if h == 0 else M - 1 - first - i
                exponent = logs_ref[order] + order.astype(F32) * log_sine
                ramp = jnp.clip((exponent + 75.0) / 10.0, 0.0, 1.0)
                start_ref[h * PAIRS + i] = jnp.exp(jnp.maximum(exponent, -75.0)) * ramp * weight
        sub = lax.broadcasted_iota(jnp.int32, (128, 256), 0) // 32
        lane = lax.broadcasted_iota(jnp.int32, (128, 256), 1) // 64
        for term in range(20):
            code = codes_ref[0, term % 4, term // 4]
            wide = jnp.dot(rmap_ref[term], rsel_ref[code], preferred_element_type=F32)
            wide = jnp.concatenate([wide] * 4, axis=0)
            rmat_out[term] = jnp.where(sub == lane, wide, 0.0).astype(BF16)
            cols_out[term] = jnp.dot(csel_ref[code], cmap_ref[term], preferred_element_type=F32).astype(BF16)

    cosine = colat_ref[0]

    def advance(base, state, switching):
        state = list(state)
        for k in range(16):
            slot = base + k
            for i in range(PAIRS):
                one, two = state[2 * i], state[2 * i + 1]
                grow = coef_ref[0, (2 * i) * STEPS + slot]
                back = coef_ref[0, (2 * i + 1) * STEPS + slot]
                value = (cosine * grow) * one - two * back
                if switching:
                    value = jnp.where(slot == 0, start_ref[i], value)
                    value = jnp.where(slot == M - first - i, start_ref[PAIRS + i], value)
                state[2 * i], state[2 * i + 1] = value, one
                rows_ref[i, k * 8 : (k + 1) * 8, :] = value
        return tuple(state)

    def sixteen(part, state):
        base = step * CHUNK + part * 16
        switching = (base == 0) | ((base <= M - first) & (base + 16 > M - first - PAIRS))
        state = lax.cond(
            switching, lambda x: advance(base, x, True), lambda x: advance(base, x, False), state
        )
        at = pl.ds(pl.multiple_of(part * 16, 16), 16)
        for i in range(PAIRS):
            for b in range(5):
                value = rows_ref[i, pl.ds(b, 16, stride=8), :]
                high = value.astype(BF16)
                high_out[i, at, b * 128 : (b + 1) * 128] = high
                low_out[i, at, b * 128 : (b + 1) * 128] = (value - high.astype(F32)).astype(BF16)
        return state

    state = lax.fori_loop(0, CHUNK // 16, sixteen, tuple(state_ref[j] for j in range(2 * PAIRS)))
    for j in range(2 * PAIRS):
        state_ref[j] = state[j]


def sums_kernel(first_ref, blocks_ref, high_hbm, low_hbm, out_ref, high_ref, low_ref, sems, spread_ref, turned_ref, left_ref):
    step = pl.program_id(0)

    def load(g):
        return (
            pltpu.make_async_copy(high_hbm.at[g], high_ref.at[g], sems.at[g]),
            pltpu.make_async_copy(low_hbm.at[g], low_ref.at[g], sems.at[PAIRS + g]),
        )

    @pl.when(step == 0)
    def _():
        for g in range(PAIRS):
            for move in load(g):
                move.start()
        lane = lax.broadcasted_iota(jnp.int32, (8, 128), 1)
        for d in range(128):
            spread_ref[d * 16 : (d + 1) * 16, :] = blocks_ref[d].astype(F32)
        for k in range(13):
            parts = [spread_ref[pl.ds(l * 256 + k, 16, stride=16), :] for l in (0, 1, 2, 3, 7, 6, 5, 4)]
            turned_ref[k * 128 : (k + 1) * 128, :] = jnp.concatenate(parts, axis=0).T
        for i in range(PAIRS):
            for h in range(2):
                for b in range(5):
                    north, south = [], []
                    for c in range(2):
                        base = SLOT[(i, h, c)] * 80 + b * 16
                        one, two = turned_ref[base : base + 8, :], turned_ref[base + 8 : base + 16, :]
                        north.append(jnp.where(lane < 64, one, pltpu.roll(two, 64, 1)))
                        south.append(jnp.where(lane < 64, pltpu.roll(one, 64, 1), two))
                    at = slice(b * 128, (b + 1) * 128)
                    left_ref[i, h * 16 : h * 16 + 16, at] = jnp.concatenate(north, axis=0).astype(BF16)
                    left_ref[i, 32 + h * 16 : 48 + h * 16, at] = jnp.concatenate(south, axis=0).astype(BF16)

    for move in load(step):
        move.wait()
    left = left_ref[step]
    both_last = (((1,), (1,)), ((), ()))
    sums = lax.dot_general(left, high_ref[step], both_last, preferred_element_type=F32)
    sums += lax.dot_general(left, low_ref[step], both_last, preferred_element_type=F32)
    pair = first_ref[0] + step
    slot = lax.broadcasted_iota(jnp.int32, (16, STEPS), 1)
    low = sums[0:16] + jnp.where(slot & 1 == 0, sums[32:48], -sums[32:48])
    high = sums[16:32] + jnp.where((slot + pair) & 1 == 0, sums[48:64], -sums[48:64])
    result = jnp.where(slot < M - pair, low, high)
    out_ref[0] = result[:, : M + 1]


def vmem(shape=None, index=None):
    if shape is None:
        return pl.BlockSpec(memory_space=pltpu.VMEM)
    return pl.BlockSpec(shape, index)


SMEM = pl.BlockSpec(memory_space=pltpu.SMEM)
HBM = pl.BlockSpec(memory_space=pltpu.HBM)


def params(limit):
    return pltpu.CompilerParams(vmem_limit_bytes=limit * MIB)


def cost(flops, moved):
    return pl.CostEstimate(flops=flops, bytes_accessed=moved, transcendentals=0)


def recurrence_factors():
    pair = np.arange(M // 2)[:, None]
    slot = np.arange(STEPS)[None, :]
    is_low = slot < M - pair
    order = np.where(is_low, pair, M - 1 - pair)
    degree = np.where(is_low, pair + slot, slot - 1)
    grows = (degree > order) & (slot <= M)
    back = (degree - 1 > order) & (slot <= M)
    n2, l2, m2 = degree.astype(np.float64) ** 2, (degree - 1.0) ** 2, order.astype(np.float64) ** 2
    grow = np.where(grows, np.sqrt(np.where(grows, 4 * n2 - 1, 0) / np.where(grows, n2 - m2, 1)), 0)
    keep = np.where(back, grow * np.sqrt(np.where(back, l2 - m2, 0) / np.where(back, 4 * l2 - 1, 1)), 0)
    return np.stack([grow, keep], axis=1).astype(np.float32).reshape(128, 1, 10 * STEPS)


def selections():
    packed = np.arange(64) % 32 * 2 + np.arange(64) // 32
    rsel, csel = np.zeros((4, 64, 256)), np.zeros((4, 128, 64))
    for code in range(4):
        rows = np.arange(64) if code % 2 else packed
        rows = 63 - rows if code in (1, 2) else rows
        for lev in range(4):
            rsel[code, rows, lev * 64 + np.arange(64)] = 1
        cols = packed if code % 2 else np.arange(64)
        cols = 63 - cols if code in (2, 3) else cols
        csel[code, np.arange(64), cols] = 1
        if code % 2 == 0:
            csel[code, 64 + np.arange(64), cols] = 1
    return rsel.astype(BF16), csel.astype(BF16)


def legendre_table(device, codes, row_map, col_map):
    terms = 0.5 * np.log1p(0.5 / np.arange(1, M, dtype=np.float64))
    logs = (np.concatenate([np.zeros(1), np.cumsum(terms)]) + 0.5 * math.log(0.5)).astype(np.float32)
    colat = latitudes()
    weight = np.pi * np.sin(colat) * math.sqrt(NLAT) / (NLAT + 0.5)
    colat = np.stack([np.cos(colat), np.log(np.sin(colat)), weight]).astype(np.float32)
    rsel, csel = selections()
    shape = (PAIRS, STEPS, 640)
    block = vmem((PAIRS, CHUNK, 640), lambda g, d: (0, g, 0))
    cols = (20, 128, 160)
    rmat = (20, 128, 256)
    whole = lambda g, d: (0, 0, 0)
    own = pl.BlockSpec((None, 1, 10 * STEPS), lambda g, d: (d[0], 0, 0), memory_space=pltpu.SMEM)
    return pl.pallas_call(
        table_kernel,
        out_shape=tuple(jax.ShapeDtypeStruct(made, BF16) for made in (shape, shape, cols, rmat)),
        grid_spec=pltpu.PrefetchScalarGridSpec(
            num_scalar_prefetch=1,
            grid=(STEPS // CHUNK,),
            in_specs=[SMEM, SMEM, own] + [vmem()] * 5,
            out_specs=(block, block, vmem(cols, whole), vmem(rmat, whole)),
            scratch_shapes=[
                pltpu.VMEM((2 * PAIRS, 8, 128), F32),
                pltpu.VMEM((2 * PAIRS, 8, 128), F32),
                pltpu.VMEM((PAIRS, 128, 128), F32),
            ],
        ),
        compiler_params=params(57),
        cost_estimate=cost(60_000_000, 60_000_000),
        name="legendre_table",
    )(
        device, codes, jnp.asarray(logs), jnp.asarray(recurrence_factors()), jnp.asarray(colat), row_map, col_map,
        jnp.asarray(rsel), jnp.asarray(csel),
    )


def body(source, row_map, col_map, pattern, codes, need_list, owner):
    lat_me = lax.axis_index("lat").astype(jnp.int32)
    tile_me = lax.axis_index("tile").astype(jnp.int32)
    device = tile_me * lax.axis_size("lat") + lat_me
    first = device * PAIRS
    me = lat_me.reshape(1)
    needs = need_list[0]
    outgoing = pl.pallas_call(
        pack_kernel,
        out_shape=jax.ShapeDtypeStruct((8 * MOST, 64, 512), BF16),
        in_specs=[SMEM, SMEM, SMEM, HBM],
        out_specs=vmem(),
        scratch_shapes=[
            pltpu.VMEM((7, 8, 4096), BF16),
            pltpu.VMEM((2, 256, 128), F32),
            pltpu.VMEM((7, 64, 512), BF16),
            pltpu.SMEM((8 * MOST + 1,), jnp.int32),
            pltpu.SemaphoreType.DMA((7,)),
        ],
        compiler_params=params(57),
        cost_estimate=cost(1_000_000, 2_000_000),
        name="pack",
    )(owner, needs, me, source)
    incoming = lax.all_to_all(outgoing, "lat", split_axis=0, concat_axis=0, tiled=True)

    code = jnp.transpose(codes, (1, 2, 0))
    table_high, table_low = (jnp.asarray(t) for t in dft_tables())
    high, low, cols, rmat = legendre_table(
        device.reshape(1), code, row_map.reshape(20, 32, 64), col_map.reshape(20, 64, 160)
    )

    field = pl.pallas_call(
        regrid_kernel,
        out_shape=jax.ShapeDtypeStruct((16, 112, 128), BF16),
        in_specs=[SMEM] * 5 + [HBM] * 3,
        out_specs=vmem(),
        scratch_shapes=[
            pltpu.VMEM((NEED, 64, 512), BF16),
            pltpu.VMEM((20, 128, 160), BF16),
            pltpu.VMEM((20, 128, 256), BF16),
            pltpu.SemaphoreType.DMA((NEED + 2,)),
            pltpu.VMEM((2 * NEED, 512, 128), BF16),
            pltpu.VMEM((2, 256, 128), F32),
            pltpu.VMEM((2, 256, 128), F32),
            pltpu.VMEM((16, 16, 128), F32),
            pltpu.SMEM((8,), jnp.int32),
        ],
        compiler_params=params(57),
        cost_estimate=cost(700_000_000, 5_000_000),
        name="regrid",
    )(owner, needs, me, jnp.transpose(pattern, (1, 2, 0)), code, incoming, cols, rmat)
    rows = lax.all_to_all(field, "tile", split_axis=0, concat_axis=0, tiled=True)

    spectral = pl.pallas_call(
        dft_kernel,
        grid=(5,),
        out_shape=jax.ShapeDtypeStruct((128, 16, 128), BF16),
        in_specs=[vmem(), HBM, HBM],
        out_specs=vmem((128, 16, 128), lambda g: (0, 0, 0)),
        scratch_shapes=[
            pltpu.VMEM((5, 2, 1280, 256), BF16),
            pltpu.VMEM((5, 2, 1280, 256), BF16),
            pltpu.SemaphoreType.DMA((10,)),
            pltpu.VMEM((2, 160, 1280), BF16),
            pltpu.VMEM((1664, 128), F32),
            pltpu.VMEM((2048, 128), F32),
        ],
        compiler_params=params(57),
        cost_estimate=cost(1_000_000_000, 14_000_000),
        name="dft",
    )(rows, table_high, table_low)
    arranged = lax.all_to_all(spectral, ("lat", "tile"), split_axis=0, concat_axis=0, tiled=True)

    return pl.pallas_call(
        sums_kernel,
        grid=(PAIRS,),
        out_shape=jax.ShapeDtypeStruct((PAIRS, 2 * LEV, M + 1), F32),
        in_specs=[SMEM, vmem(), HBM, HBM],
        out_specs=vmem((1, 2 * LEV, M + 1), lambda g: (g, 0, 0)),
        scratch_shapes=[
            pltpu.VMEM((PAIRS, STEPS, 640), BF16),
            pltpu.VMEM((PAIRS, STEPS, 640), BF16),
            pltpu.SemaphoreType.DMA((2 * PAIRS,)),
            pltpu.VMEM((2048, 128), F32),
            pltpu.VMEM((1664, 128), F32),
            pltpu.VMEM((PAIRS, 64, 640), BF16),
        ],
        compiler_params=params(57),
        cost_estimate=cost(2_000_000_000, 17_000_000),
        name="sums",
    )(first.reshape(1), arranged, high, low)


def solution(mesh):
    placed = (
        P(("tile", "lat"), None, None),
        P("lat", "tile", None, None, None),
        P("lat", None, None, "tile"),
        P("lat", "tile", None),
        P("lat", "tile", None),
        P("tile", None, None),
        P(),
    )
    return jax.shard_map(
        body, mesh=mesh, in_specs=placed, out_specs=P(("tile", "lat"), None, None), check_vma=False
    )
```

```python
import math

import jax
import jax.numpy as jnp
import numpy as np
from jax import lax
from jax.experimental import pallas as pl
from jax.experimental.pallas import tpu as pltpu
from jax.sharding import PartitionSpec as P

NLON = 2560
NLAT = 1280
M = 1280
NEED = 12
MOST = 3
LEV = 8
PAIRS = 5
STEPS = 1296
CHUNK = 144
MIB = 2**20
F32 = jnp.float32
BF16 = jnp.bfloat16

EVENS = [(i, h, c) for i in range(5) for h in range(2) if (i + h) % 2 == 0 for c in range(2)]
ODDS = [(i, h, c) for i in range(5) for h in range(2) if (i + h) % 2 == 1 for c in range(2)]
SLOT = {e: 2 * w for w, e in enumerate(EVENS)} | {e: 2 * w + 1 for w, e in enumerate(ODDS)}


def dft_tables():
    s = np.arange(8)
    points = np.concatenate(
        [(s[:, None] * 160 + np.arange(128)).ravel(), (s[:, None] * 160 + np.arange(128, 160)).ravel()]
    )
    l2, t = np.meshgrid(np.arange(4), np.arange(16), indexing="ij")
    order = np.zeros((2, 10, 2, 64), np.int64)
    part = np.zeros((2, 10, 2, 64), np.int64)
    for q in range(2):
        for w in range(10):
            for half in range(2):
                i, h, c = (EVENS if q == half else ODDS)[w]
                pair = 5 * (t * 8 + 2 * l2 + half) + i
                order[q, w, half] = (pair if h == 0 else M - 1 - pair).ravel()
                part[q, w, half] = c
    order, part = order.reshape(2, 1, 1280), part.reshape(2, 1, 1280)
    angle = (points[None, :, None] * order % NLON) * (2.0 * np.pi / NLON)
    table = np.where(part == 0, np.cos(angle), -np.sin(angle)) / math.sqrt(NLON)
    high = table.astype(BF16)
    low = (table - high.astype(np.float64)).astype(BF16)
    both = np.stack([x.reshape(2, 1280, 5, 256).transpose(2, 0, 1, 3) for x in (high, low)], axis=1)
    return np.ascontiguousarray(both)


def latitudes():
    b, a2, l, t = np.meshgrid(np.arange(5), np.arange(2), np.arange(4), np.arange(16), indexing="ij")
    lat = (l * 160 + b * 32 + 2 * t + a2).reshape(5, 128)
    colat = np.pi * (lat + 0.75) / (NLAT + 0.5)
    return np.concatenate([colat, np.full((3, 128), np.pi / 2)])


def holder_of(owner_ref, need_ref, dest, i):
    holder = owner_ref[need_ref[dest, i]]
    device = (holder * 9363) >> 16
    return device & 7, holder - 7 * device


def pack_kernel(owner_ref, need_ref, me_ref, source_hbm, out_hbm, source_ref, rows_ref, turned_ref, list_ref, sems):
    loads = [pltpu.make_async_copy(source_hbm.at[s], source_ref.at[s], sems.at[s]) for s in range(7)]
    for load in loads:
        load.start()
    lane = lax.broadcasted_iota(jnp.int32, (32, 128), 1)
    me = me_ref[0]
    for at in range(8 * MOST):
        list_ref[at] = 0
    for dest in range(8):
        count = jnp.int32(0)
        for i in range(NEED):
            lat, slot = holder_of(owner_ref, need_ref, dest, i)
            hit = lat == me
            list_ref[jnp.where(hit, dest * MOST + jnp.minimum(count, MOST - 1), 8 * MOST)] = slot
            count = count + hit.astype(jnp.int32)
    for s in range(7):
        loads[s].wait()
        for i in range(32):
            rows_ref[s % 2, pl.ds(i, 8, stride=32), :] = source_ref[s, :, i * 128 : (i + 1) * 128].astype(F32)
        for lp in range(4):
            one = rows_ref[s % 2, lp * 64 : lp * 64 + 32, :]
            two = rows_ref[s % 2, lp * 64 + 32 : lp * 64 + 64, :]
            top = jnp.where(lane < 64, one, pltpu.roll(two, 64, 1))
            low = jnp.where(lane < 64, pltpu.roll(one, 64, 1), two)
            at = slice(lp * 128, (lp + 1) * 128)
            turned_ref[s, 0:32, at] = top.astype(BF16)
            turned_ref[s, 32:64, at] = low.astype(BF16)
    stores = [
        pltpu.make_async_copy(turned_ref.at[list_ref[at]], out_hbm.at[at], sems.at[7 + at]) for at in range(8 * MOST)
    ]
    for store in stores:
        store.start()
    for store in stores:
        store.wait()


def regrid_kernel(
    owner_ref, need_ref, me_ref, pattern_ref, codes_ref, blocks_ref, maps_hbm, out_ref,
    maps_ref, sems, forms_ref, acc_ref, tail_ref, packed_ref, seen_ref,
):
    me = me_ref[0]
    south = me >= 4
    row_blocks = [jnp.where(south, 4 - b, b) for b in range(5)]
    loads = [
        pltpu.make_async_copy(maps_hbm.at[pl.ds(row_blocks[b] * 4, 4)], maps_ref.at[b * 4 : b * 4 + 4], sems.at[b])
        for b in range(5)
    ]
    for load in loads:
        load.start()
    for l in range(8):
        seen_ref[l] = 0
    tail_ref[...] = jnp.zeros_like(tail_ref)
    lane = lax.broadcasted_iota(jnp.int32, (64, 128), 1)
    zero = jnp.zeros((64, 128), BF16)
    places = []
    for i in range(NEED):
        lat, _ = holder_of(owner_ref, need_ref, me, i)
        rank = seen_ref[lat]
        at = lat * MOST + jnp.minimum(rank, MOST - 1)
        seen_ref[lat] = rank + 1
        places.append(at)
    for i in range(NEED):
        for lp in range(0, 4, 2):
            tiles = [blocks_ref[places[i], :, (lp + j) * 128 : (lp + j + 1) * 128] for j in range(2)]
            both = jnp.concatenate(tiles, axis=0).astype(F32).T.astype(BF16)
            for j, tile in enumerate(tiles):
                at = (lp + j) * 128
                forms_ref[2 * i, at : at + 64, :] = jnp.where(lane < 64, tile, zero)
                forms_ref[2 * i, at + 64 : at + 128, :] = jnp.where(lane < 64, zero, tile)
                for half in range(2):
                    part = both[half * 64 : half * 64 + 64]
                    picked = jnp.where(lane < 64, part, zero) if j == 0 else jnp.where(lane < 64, zero, part)
                    forms_ref[2 * i + 1, at + half * 64 : at + half * 64 + 64, :] = picked

    for b in range(5):
        loads[b].wait()
        sums = [None, None]
        for k in range(4):
            term = b * 4 + k
            form = forms_ref[pattern_ref[0, k, row_blocks[b]] * 2 + (codes_ref[0, k, row_blocks[b]] & 1)]
            inner = jnp.dot(form, maps_ref[term, :, 0:160], preferred_element_type=F32).astype(BF16)
            for half in range(2):
                new = jnp.dot(
                    maps_ref[term, :, 256:512], inner[half * 256 : (half + 1) * 256], preferred_element_type=F32
                )
                sums[half] = new if k == 0 else sums[half] + new
        for half in range(2):
            acc_ref[b % 2, half * 128 : (half + 1) * 128, :] = sums[half][:, :128]
            tail_ref[b % 2, half * 128 : (half + 1) * 128, 0:32] = sums[half][:, 128:160]
        for t in range(16):
            at = [jnp.where(south, 31 - (2 * t + a), 2 * t + a) for a in range(2)]
            main = [acc_ref[b % 2, pl.ds(at[a], 8, stride=32), :] for a in range(2)]
            out_ref[t, b * 16 : (b + 1) * 16, :] = jnp.concatenate(main, axis=0).astype(BF16)
            rest = jnp.concatenate([tail_ref[b % 2, pl.ds(at[a], 8, stride=32), :] for a in range(2)], axis=0)
            if b == 0:
                packed_ref[t] = rest
            elif b < 4:
                packed_ref[t] += pltpu.roll(rest, 32 * b, 1)
            else:
                out_ref[t, 96:112, :] = rest.astype(BF16)
    for t in range(16):
        out_ref[t, 80:96, :] = packed_ref[t].astype(BF16)


def dft_kernel(rows_ref, table_hbm, out_ref, table_ref, sems, both_ref, sums_ref, spread_ref):
    lane = lax.broadcasted_iota(jnp.int32, (80, 128), 1)
    loads = [pltpu.make_async_copy(table_hbm.at[g], table_ref.at[g], sems.at[g]) for g in range(5)]
    for load in loads:
        load.start()
    quarter = lax.broadcasted_iota(jnp.int32, (16, 128), 1) // 32
    sums_ref[1600:1664, :] = jnp.zeros((64, 128), F32)
    for q in range(2):

        def mixed(s, at):
            one, two = rows_ref[s, at, :].astype(F32), rows_ref[s + 8, at, :].astype(F32)
            return one + two if q == 0 else one - two

        def put(row, count, at, value):
            high = value.astype(BF16)
            both_ref[q, row : row + count, at] = high
            both_ref[q, 80 + row : 80 + row + count, at] = (value - high.astype(F32)).astype(BF16)

        for s in range(8):
            put(0, 80, slice(s * 128, (s + 1) * 128), mixed(s, slice(0, 80)))
        for group in range(2):
            first = [mixed(group * 4 + j, slice(80, 96)) for j in range(4)]
            last = [mixed(group * 4 + j, slice(96, 112)) for j in range(4)]
            for b in range(5):
                value = jnp.zeros((16, 128), F32)
                for j in range(4):
                    tile = first[j] if b < 4 else last[j]
                    shift = (32 * (j - (b if b < 4 else 0))) % 128
                    moved = tile if shift == 0 else pltpu.roll(tile, shift, 1)
                    value = jnp.where(quarter == j, moved, value)
                put(b * 16, 16, slice(1024 + group * 128, 1152 + group * 128), value)

    for step in range(5):
        loads[step].wait()
        outs = []
        for q in range(2):
            main = jnp.dot(both_ref[q], table_ref[step, 0, q], preferred_element_type=F32)
            rest = jnp.dot(both_ref[q, 0:80, :], table_ref[step, 1, q], preferred_element_type=F32)
            outs.append(main[0:80] + main[80:160] + rest)
        for half in range(2):
            at = slice(half * 128, (half + 1) * 128)
            even = jnp.where(lane < 64, outs[0][:, at], outs[1][:, at])
            odd = jnp.where(lane < 64, outs[1][:, at], outs[0][:, at])
            base = step * 320 + half * 160
            sums_ref[base : base + 80, :] = even
            sums_ref[base + 80 : base + 160, :] = odd
    for k in range(13):
        turned = sums_ref[k * 128 : (k + 1) * 128, :].T
        for group in range(8):
            l = 2 * (group % 4) + group // 4
            spread_ref[pl.ds(l * 256 + k, 16, stride=16), :] = turned[group * 16 : (group + 1) * 16]
    for d in range(128):
        out_ref[d] = spread_ref[d * 16 : (d + 1) * 16, :].astype(BF16)


def table_kernel(
    device_ref, codes_ref, logs_ref, coef_ref, colat_ref, rmap_ref, cmap_ref, rsel_ref, csel_ref,
    legendre_out, maps_out, state_ref, start_ref, rows_ref,
):
    step = pl.program_id(0)
    first = device_ref[0] * PAIRS

    @pl.when(step == 0)
    def _():
        state_ref[...] = jnp.zeros_like(state_ref)
        log_sine, weight = colat_ref[1], colat_ref[2]
        for i in range(PAIRS):
            for h in range(2):
                order = first + i if h == 0 else M - 1 - first - i
                exponent = logs_ref[order] + order.astype(F32) * log_sine
                ramp = jnp.clip((exponent + 75.0) / 10.0, 0.0, 1.0)
                start_ref[h * PAIRS + i] = jnp.exp(jnp.maximum(exponent, -75.0)) * ramp * weight
        sub = lax.broadcasted_iota(jnp.int32, (128, 256), 0) // 32
        lane = lax.broadcasted_iota(jnp.int32, (128, 256), 1) // 64
        for term in range(20):
            code = codes_ref[0, term % 4, term // 4]
            wide = jnp.dot(rmap_ref[term], rsel_ref[code], preferred_element_type=F32)
            wide = jnp.concatenate([wide] * 4, axis=0)
            maps_out[term, :, 256:512] = jnp.where(sub == lane, wide, 0.0).astype(BF16)
            maps_out[term, :, 0:160] = jnp.dot(csel_ref[code], cmap_ref[term], preferred_element_type=F32).astype(BF16)

    cosine = colat_ref[0]

    def advance(base, state, switching):
        state = list(state)
        for k in range(16):
            slot = base + k
            for i in range(PAIRS):
                one, two = state[2 * i], state[2 * i + 1]
                grow = coef_ref[0, (2 * i) * STEPS + slot]
                back = coef_ref[0, (2 * i + 1) * STEPS + slot]
                value = (cosine * grow) * one - two * back
                if switching:
                    value = jnp.where(slot == 0, start_ref[i], value)
                    value = jnp.where(slot == M - first - i, start_ref[PAIRS + i], value)
                state[2 * i], state[2 * i + 1] = value, one
                rows_ref[i, k * 8 : (k + 1) * 8, :] = value
        return tuple(state)

    def sixteen(part, state):
        base = step * CHUNK + part * 16
        switching = (base == 0) | ((base <= M - first) & (base + 16 > M - first - PAIRS))
        state = lax.cond(
            switching, lambda x: advance(base, x, True), lambda x: advance(base, x, False), state
        )
        at = pl.ds(pl.multiple_of(part * 16, 16), 16)
        for i in range(PAIRS):
            for b in range(5):
                value = rows_ref[i, pl.ds(b, 16, stride=8), :]
                high = value.astype(BF16)
                legendre_out[i, at, b * 128 : (b + 1) * 128] = high
                legendre_out[i, at, 640 + b * 128 : 768 + b * 128] = (value - high.astype(F32)).astype(BF16)
        return state

    state = lax.fori_loop(0, CHUNK // 16, sixteen, tuple(state_ref[j] for j in range(2 * PAIRS)))
    for j in range(2 * PAIRS):
        state_ref[j] = state[j]


def sums_kernel(
    first_ref, blocks_ref, table_hbm, out_hbm, table_ref, out_ref, sems, spread_ref, turned_ref, left_ref,
):
    loads = [pltpu.make_async_copy(table_hbm.at[i], table_ref.at[i], sems.at[i]) for i in range(PAIRS)]
    stores = [pltpu.make_async_copy(out_ref.at[i], out_hbm.at[i], sems.at[PAIRS + i]) for i in range(PAIRS)]
    for load in loads:
        load.start()
    lane = lax.broadcasted_iota(jnp.int32, (8, 128), 1)
    for d in range(128):
        spread_ref[d * 16 : (d + 1) * 16, :] = blocks_ref[d].astype(F32)
    for k in range(13):
        parts = [spread_ref[pl.ds(l * 256 + k, 16, stride=16), :] for l in (0, 1, 2, 3, 7, 6, 5, 4)]
        turned_ref[k * 128 : (k + 1) * 128, :] = jnp.concatenate(parts, axis=0).T
    for i in range(PAIRS):
        for h in range(2):
            for b in range(5):
                north, south = [], []
                for c in range(2):
                    base = SLOT[(i, h, c)] * 80 + b * 16
                    one, two = turned_ref[base : base + 8, :], turned_ref[base + 8 : base + 16, :]
                    north.append(jnp.where(lane < 64, one, pltpu.roll(two, 64, 1)))
                    south.append(jnp.where(lane < 64, pltpu.roll(one, 64, 1), two))
                at, again = slice(b * 128, (b + 1) * 128), slice(640 + b * 128, 768 + b * 128)
                north = jnp.concatenate(north, axis=0).astype(BF16)
                left_ref[i, h * 16 : h * 16 + 16, at] = north
                left_ref[i, h * 16 : h * 16 + 16, again] = north
                south = jnp.concatenate(south, axis=0).astype(BF16)
                left_ref[i, 32 + h * 16 : 48 + h * 16, at] = south
                left_ref[i, 32 + h * 16 : 48 + h * 16, again] = south

    slot = lax.broadcasted_iota(jnp.int32, (16, STEPS), 1)
    for i in range(PAIRS):
        loads[i].wait()
        sums = lax.dot_general(left_ref[i], table_ref[i], (((1,), (1,)), ((), ())), preferred_element_type=F32)
        pair = first_ref[0] + i
        low = sums[0:16] + jnp.where(slot & 1 == 0, sums[32:48], -sums[32:48])
        high = sums[16:32] + jnp.where((slot + pair) & 1 == 0, sums[48:64], -sums[48:64])
        result = jnp.where(slot < M - pair, low, high)
        out_ref[i] = result[:, : M + 1]
        stores[i].start()
    for store in stores:
        store.wait()


def vmem(shape=None, index=None):
    if shape is None:
        return pl.BlockSpec(memory_space=pltpu.VMEM)
    return pl.BlockSpec(shape, index)


SMEM = pl.BlockSpec(memory_space=pltpu.SMEM)
HBM = pl.BlockSpec(memory_space=pltpu.HBM)


def params(limit):
    return pltpu.CompilerParams(vmem_limit_bytes=limit * MIB)


def cost(flops, moved):
    return pl.CostEstimate(flops=flops, bytes_accessed=moved, transcendentals=0)


def recurrence_factors():
    pair = np.arange(M // 2)[:, None]
    slot = np.arange(STEPS)[None, :]
    is_low = slot < M - pair
    order = np.where(is_low, pair, M - 1 - pair)
    degree = np.where(is_low, pair + slot, slot - 1)
    grows = (degree > order) & (slot <= M)
    back = (degree - 1 > order) & (slot <= M)
    n2, l2, m2 = degree.astype(np.float64) ** 2, (degree - 1.0) ** 2, order.astype(np.float64) ** 2
    grow = np.where(grows, np.sqrt(np.where(grows, 4 * n2 - 1, 0) / np.where(grows, n2 - m2, 1)), 0)
    keep = np.where(back, grow * np.sqrt(np.where(back, l2 - m2, 0) / np.where(back, 4 * l2 - 1, 1)), 0)
    return np.stack([grow, keep], axis=1).astype(np.float32).reshape(128, 1, 10 * STEPS)


def selections():
    packed = np.arange(64) % 32 * 2 + np.arange(64) // 32
    rsel, csel = np.zeros((4, 64, 256)), np.zeros((4, 128, 64))
    for code in range(4):
        rows = np.arange(64) if code % 2 else packed
        rows = 63 - rows if code in (1, 2) else rows
        for lev in range(4):
            rsel[code, rows, lev * 64 + np.arange(64)] = 1
        cols = packed if code % 2 else np.arange(64)
        cols = 63 - cols if code in (2, 3) else cols
        csel[code, np.arange(64), cols] = 1
        csel[code, 64 + np.arange(64), cols] = 1
    return rsel.astype(BF16), csel.astype(BF16)


def legendre_table(device, codes, row_map, col_map):
    terms = 0.5 * np.log1p(0.5 / np.arange(1, M, dtype=np.float64))
    logs = (np.concatenate([np.zeros(1), np.cumsum(terms)]) + 0.5 * math.log(0.5)).astype(np.float32)
    colat = latitudes()
    weight = np.pi * np.sin(colat) * math.sqrt(NLAT) / (NLAT + 0.5)
    colat = np.stack([np.cos(colat), np.log(np.sin(colat)), weight]).astype(np.float32)
    rsel, csel = selections()
    table = (PAIRS, STEPS, 1280)
    block = vmem((PAIRS, CHUNK, 1280), lambda g, d: (0, g, 0))
    maps = (20, 128, 512)
    whole = lambda g, d: (0, 0, 0)
    own = pl.BlockSpec((None, 1, 10 * STEPS), lambda g, d: (d[0], 0, 0), memory_space=pltpu.SMEM)
    return pl.pallas_call(
        table_kernel,
        out_shape=tuple(jax.ShapeDtypeStruct(made, BF16) for made in (table, maps)),
        grid_spec=pltpu.PrefetchScalarGridSpec(
            num_scalar_prefetch=1,
            grid=(STEPS // CHUNK,),
            in_specs=[SMEM, SMEM, own] + [vmem()] * 5,
            out_specs=(block, vmem(maps, whole)),
            scratch_shapes=[
                pltpu.VMEM((2 * PAIRS, 8, 128), F32),
                pltpu.VMEM((2 * PAIRS, 8, 128), F32),
                pltpu.VMEM((PAIRS, 128, 128), F32),
            ],
        ),
        compiler_params=params(57),
        cost_estimate=cost(60_000_000, 60_000_000),
        name="legendre_table",
    )(
        device, codes, jnp.asarray(logs), jnp.asarray(recurrence_factors()), jnp.asarray(colat), row_map, col_map,
        jnp.asarray(rsel), jnp.asarray(csel),
    )


def body(source, row_map, col_map, pattern, codes, need_list, owner):
    lat_me = lax.axis_index("lat").astype(jnp.int32)
    tile_me = lax.axis_index("tile").astype(jnp.int32)
    device = tile_me * lax.axis_size("lat") + lat_me
    first = device * PAIRS
    me = lat_me.reshape(1)
    needs = need_list[0]
    outgoing = pl.pallas_call(
        pack_kernel,
        out_shape=jax.ShapeDtypeStruct((8 * MOST, 64, 512), BF16),
        in_specs=[SMEM, SMEM, SMEM, HBM],
        out_specs=HBM,
        scratch_shapes=[
            pltpu.VMEM((7, 8, 4096), BF16),
            pltpu.VMEM((2, 256, 128), F32),
            pltpu.VMEM((7, 64, 512), BF16),
            pltpu.SMEM((8 * MOST + 1,), jnp.int32),
            pltpu.SemaphoreType.DMA((7 + 8 * MOST,)),
        ],
        compiler_params=params(57),
        cost_estimate=cost(1_000_000, 2_000_000),
        name="pack",
    )(owner, needs, me, source)
    incoming = lax.all_to_all(outgoing, "lat", split_axis=0, concat_axis=0, tiled=True)

    code = jnp.transpose(codes, (1, 2, 0))
    table, maps = legendre_table(
        device.reshape(1), code, row_map.reshape(20, 32, 64), col_map.reshape(20, 64, 160)
    )

    field = pl.pallas_call(
        regrid_kernel,
        out_shape=jax.ShapeDtypeStruct((16, 112, 128), BF16),
        in_specs=[SMEM] * 5 + [vmem(), HBM],
        out_specs=vmem(),
        scratch_shapes=[
            pltpu.VMEM((20, 128, 512), BF16),
            pltpu.SemaphoreType.DMA((5,)),
            pltpu.VMEM((2 * NEED, 512, 128), BF16),
            pltpu.VMEM((2, 256, 128), F32),
            pltpu.VMEM((2, 256, 128), F32),
            pltpu.VMEM((16, 16, 128), F32),
            pltpu.SMEM((8,), jnp.int32),
        ],
        compiler_params=params(50),
        cost_estimate=cost(700_000_000, 5_000_000),
        name="regrid",
    )(owner, needs, me, jnp.transpose(pattern, (1, 2, 0)), code, incoming, maps)
    rows = lax.all_to_all(field, "tile", split_axis=0, concat_axis=0, tiled=True)

    spectral = pl.pallas_call(
        dft_kernel,
        out_shape=jax.ShapeDtypeStruct((128, 16, 128), BF16),
        in_specs=[vmem(), HBM],
        out_specs=vmem(),
        scratch_shapes=[
            pltpu.VMEM((5, 2, 2, 1280, 256), BF16),
            pltpu.SemaphoreType.DMA((5,)),
            pltpu.VMEM((2, 160, 1280), BF16),
            pltpu.VMEM((1664, 128), F32),
            pltpu.VMEM((2048, 128), F32),
        ],
        compiler_params=params(50),
        cost_estimate=cost(1_000_000_000, 14_000_000),
        name="dft",
    )(rows, jnp.asarray(dft_tables()))
    arranged = lax.all_to_all(spectral, ("lat", "tile"), split_axis=0, concat_axis=0, tiled=True)

    return pl.pallas_call(
        sums_kernel,
        out_shape=jax.ShapeDtypeStruct((PAIRS, 2 * LEV, M + 1), F32),
        in_specs=[SMEM, vmem(), HBM],
        out_specs=HBM,
        scratch_shapes=[
            pltpu.VMEM((PAIRS, STEPS, 1280), BF16),
            pltpu.VMEM((PAIRS, 2 * LEV, M + 1), F32),
            pltpu.SemaphoreType.DMA((2 * PAIRS,)),
            pltpu.VMEM((2048, 128), F32),
            pltpu.VMEM((1664, 128), F32),
            pltpu.VMEM((PAIRS, 64, 1280), BF16),
        ],
        compiler_params=params(50),
        cost_estimate=cost(2_000_000_000, 17_000_000),
        name="sums",
    )(first.reshape(1), arranged, table)


def solution(mesh):
    placed = (
        P(("tile", "lat"), None, None),
        P("lat", "tile", None, None, None),
        P("lat", None, None, "tile"),
        P("lat", "tile", None),
        P("lat", "tile", None),
        P("tile", None, None),
        P(),
    )
    return jax.shard_map(
        body, mesh=mesh, in_specs=placed, out_specs=P(("tile", "lat"), None, None), check_vma=False
    )
```

```python
import math

import jax
import jax.numpy as jnp
import numpy as np
from jax import lax
from jax.experimental import pallas as pl
from jax.experimental.pallas import tpu as pltpu
from jax.sharding import PartitionSpec as P

NLON = 2560
NLAT = 1280
M = 1280
NEED = 12
MOST = 3
LEV = 8
PAIRS = 5
STEPS = 1296
CHUNK = 144
MIB = 2**20
F32 = jnp.float32
BF16 = jnp.bfloat16

EVENS = [(i, h, c) for i in range(5) for h in range(2) if (i + h) % 2 == 0 for c in range(2)]
ODDS = [(i, h, c) for i in range(5) for h in range(2) if (i + h) % 2 == 1 for c in range(2)]
SLOT = {e: 2 * w for w, e in enumerate(EVENS)} | {e: 2 * w + 1 for w, e in enumerate(ODDS)}


def dft_tables():
    s = np.arange(8)
    points = np.concatenate(
        [(s[:, None] * 160 + np.arange(128)).ravel(), (s[:, None] * 160 + np.arange(128, 160)).ravel()]
    )
    l2, t = np.meshgrid(np.arange(4), np.arange(16), indexing="ij")
    order = np.zeros((2, 10, 2, 64), np.int64)
    part = np.zeros((2, 10, 2, 64), np.int64)
    for q in range(2):
        for w in range(10):
            for half in range(2):
                i, h, c = (EVENS if q == half else ODDS)[w]
                pair = 5 * (t * 8 + 2 * l2 + half) + i
                order[q, w, half] = (pair if h == 0 else M - 1 - pair).ravel()
                part[q, w, half] = c
    order, part = order.reshape(2, 1, 1280), part.reshape(2, 1, 1280)
    angle = (points[None, :, None] * order % NLON) * (2.0 * np.pi / NLON)
    table = np.where(part == 0, np.cos(angle), -np.sin(angle)) / math.sqrt(NLON)
    high = table.astype(BF16)
    low = (table - high.astype(np.float64)).astype(BF16)
    both = np.stack([x.reshape(2, 1280, 5, 256).transpose(2, 0, 1, 3) for x in (high, low)], axis=1)
    return np.ascontiguousarray(both)


def latitudes():
    b, a2, l, t = np.meshgrid(np.arange(5), np.arange(2), np.arange(4), np.arange(16), indexing="ij")
    lat = (l * 160 + b * 32 + 2 * t + a2).reshape(5, 128)
    colat = np.pi * (lat + 0.75) / (NLAT + 0.5)
    return np.concatenate([colat, np.full((3, 128), np.pi / 2)])


def holder_of(owner_ref, need_ref, dest, i):
    holder = owner_ref[need_ref[dest, i]]
    device = (holder * 9363) >> 16
    return device & 7, holder - 7 * device


def pack_kernel(owner_ref, need_ref, me_ref, source_hbm, out_hbm, source_ref, rows_ref, turned_ref, list_ref, sems):
    loads = [pltpu.make_async_copy(source_hbm.at[s], source_ref.at[s], sems.at[s]) for s in range(7)]
    for load in loads:
        load.start()
    lane = lax.broadcasted_iota(jnp.int32, (32, 128), 1)
    me = me_ref[0]
    for at in range(8 * MOST):
        list_ref[at] = 0
    for dest in range(8):
        count = jnp.int32(0)
        for i in range(NEED):
            lat, slot = holder_of(owner_ref, need_ref, dest, i)
            hit = lat == me
            list_ref[jnp.where(hit, dest * MOST + jnp.minimum(count, MOST - 1), 8 * MOST)] = slot
            count = count + hit.astype(jnp.int32)
    for s in range(7):
        loads[s].wait()
        for i in range(32):
            rows_ref[s % 2, pl.ds(i, 8, stride=32), :] = source_ref[s, :, i * 128 : (i + 1) * 128].astype(F32)
        for lp in range(4):
            one = rows_ref[s % 2, lp * 64 : lp * 64 + 32, :]
            two = rows_ref[s % 2, lp * 64 + 32 : lp * 64 + 64, :]
            top = jnp.where(lane < 64, one, pltpu.roll(two, 64, 1))
            low = jnp.where(lane < 64, pltpu.roll(one, 64, 1), two)
            at = slice(lp * 128, (lp + 1) * 128)
            turned_ref[s, 0:32, at] = top.astype(BF16)
            turned_ref[s, 32:64, at] = low.astype(BF16)
    stores = [
        pltpu.make_async_copy(turned_ref.at[list_ref[at]], out_hbm.at[at], sems.at[7 + at]) for at in range(8 * MOST)
    ]
    for store in stores:
        store.start()
    for store in stores:
        store.wait()


def regrid_kernel(
    owner_ref, need_ref, me_ref, pattern_ref, codes_ref, blocks_ref, cols_ref, wide_ref, out_ref,
    forms_ref, acc_ref, tail_ref, packed_ref, seen_ref,
):
    me = me_ref[0]
    south = me >= 4
    row_blocks = [jnp.where(south, 4 - b, b) for b in range(5)]
    for l in range(8):
        seen_ref[l] = 0
    tail_ref[...] = jnp.zeros_like(tail_ref)
    lane = lax.broadcasted_iota(jnp.int32, (64, 128), 1)
    zero = jnp.zeros((64, 128), BF16)
    diagonal = lax.broadcasted_iota(jnp.int32, (128, 256), 0) // 32 == lax.broadcasted_iota(jnp.int32, (128, 256), 1) // 64
    places = []
    for i in range(NEED):
        lat, _ = holder_of(owner_ref, need_ref, me, i)
        rank = seen_ref[lat]
        at = lat * MOST + jnp.minimum(rank, MOST - 1)
        seen_ref[lat] = rank + 1
        places.append(at)
    for i in range(NEED):
        for lp in range(0, 4, 2):
            tiles = [blocks_ref[places[i], :, (lp + j) * 128 : (lp + j + 1) * 128] for j in range(2)]
            both = jnp.concatenate(tiles, axis=0).astype(F32).T.astype(BF16)
            for j, tile in enumerate(tiles):
                at = (lp + j) * 128
                forms_ref[2 * i, at : at + 64, :] = jnp.where(lane < 64, tile, zero)
                forms_ref[2 * i, at + 64 : at + 128, :] = jnp.where(lane < 64, zero, tile)
                for half in range(2):
                    part = both[half * 64 : half * 64 + 64]
                    picked = jnp.where(lane < 64, part, zero) if j == 0 else jnp.where(lane < 64, zero, part)
                    forms_ref[2 * i + 1, at + half * 64 : at + half * 64 + 64, :] = picked

    for b in range(5):
        sums = [None, None]
        for k in range(4):
            term = row_blocks[b] * 4 + k
            form = forms_ref[pattern_ref[0, k, row_blocks[b]] * 2 + (codes_ref[0, k, row_blocks[b]] & 1)]
            rows = jnp.where(diagonal, jnp.concatenate([wide_ref[term]] * 4, axis=0), jnp.zeros((128, 256), BF16))
            inner = jnp.dot(form, cols_ref[term], preferred_element_type=F32).astype(BF16)
            for half in range(2):
                new = jnp.dot(rows, inner[half * 256 : (half + 1) * 256], preferred_element_type=F32)
                sums[half] = new if k == 0 else sums[half] + new
        for half in range(2):
            acc_ref[b % 2, half * 128 : (half + 1) * 128, :] = sums[half][:, :128]
            tail_ref[b % 2, half * 128 : (half + 1) * 128, 0:32] = sums[half][:, 128:160]
        for t in range(16):
            at = [jnp.where(south, 31 - (2 * t + a), 2 * t + a) for a in range(2)]
            main = [acc_ref[b % 2, pl.ds(at[a], 8, stride=32), :] for a in range(2)]
            out_ref[t, b * 16 : (b + 1) * 16, :] = jnp.concatenate(main, axis=0).astype(BF16)
            rest = jnp.concatenate([tail_ref[b % 2, pl.ds(at[a], 8, stride=32), :] for a in range(2)], axis=0)
            if b == 0:
                packed_ref[t] = rest
            elif b < 4:
                packed_ref[t] += pltpu.roll(rest, 32 * b, 1)
            else:
                out_ref[t, 96:112, :] = rest.astype(BF16)
    for t in range(16):
        out_ref[t, 80:96, :] = packed_ref[t].astype(BF16)


def dft_kernel(rows_ref, table_hbm, out_ref, table_ref, sems, both_ref, sums_ref, spread_ref):
    lane = lax.broadcasted_iota(jnp.int32, (80, 128), 1)
    loads = [pltpu.make_async_copy(table_hbm.at[g], table_ref.at[g], sems.at[g]) for g in range(5)]
    for load in loads:
        load.start()
    quarter = lax.broadcasted_iota(jnp.int32, (16, 128), 1) // 32
    sums_ref[1600:1664, :] = jnp.zeros((64, 128), F32)
    for q in range(2):

        def mixed(s, at):
            one, two = rows_ref[s, at, :].astype(F32), rows_ref[s + 8, at, :].astype(F32)
            return one + two if q == 0 else one - two

        def put(row, count, at, value):
            high = value.astype(BF16)
            both_ref[q, row : row + count, at] = high
            both_ref[q, 80 + row : 80 + row + count, at] = (value - high.astype(F32)).astype(BF16)

        for s in range(8):
            put(0, 80, slice(s * 128, (s + 1) * 128), mixed(s, slice(0, 80)))
        for group in range(2):
            first = [mixed(group * 4 + j, slice(80, 96)) for j in range(4)]
            last = [mixed(group * 4 + j, slice(96, 112)) for j in range(4)]
            for b in range(5):
                value = jnp.zeros((16, 128), F32)
                for j in range(4):
                    tile = first[j] if b < 4 else last[j]
                    shift = (32 * (j - (b if b < 4 else 0))) % 128
                    moved = tile if shift == 0 else pltpu.roll(tile, shift, 1)
                    value = jnp.where(quarter == j, moved, value)
                put(b * 16, 16, slice(1024 + group * 128, 1152 + group * 128), value)

    for step in range(5):
        loads[step].wait()
        outs = []
        for q in range(2):
            main = jnp.dot(both_ref[q], table_ref[step, 0, q], preferred_element_type=F32)
            rest = jnp.dot(both_ref[q, 0:80, :], table_ref[step, 1, q], preferred_element_type=F32)
            outs.append(main[0:80] + main[80:160] + rest)
        for half in range(2):
            at = slice(half * 128, (half + 1) * 128)
            even = jnp.where(lane < 64, outs[0][:, at], outs[1][:, at])
            odd = jnp.where(lane < 64, outs[1][:, at], outs[0][:, at])
            base = step * 320 + half * 160
            sums_ref[base : base + 80, :] = even
            sums_ref[base + 80 : base + 160, :] = odd
    for k in range(13):
        turned = sums_ref[k * 128 : (k + 1) * 128, :].T
        for group in range(8):
            l = 2 * (group % 4) + group // 4
            spread_ref[pl.ds(l * 256 + k, 16, stride=16), :] = turned[group * 16 : (group + 1) * 16]
    for d in range(128):
        out_ref[d] = spread_ref[d * 16 : (d + 1) * 16, :].astype(BF16)


def table_kernel(
    device_ref, codes_ref, coef_ref, colat_ref, rmap_ref, cmap_ref, select_ref,
    legendre_out, cols_out, wide_out, state_ref, start_ref, rows_ref,
):
    step = pl.program_id(0)
    first = device_ref[0] * PAIRS

    @pl.when(step == 0)
    def _():
        state_ref[...] = jnp.zeros_like(state_ref)
        log_sine, weight = colat_ref[1], colat_ref[2]
        for i in range(PAIRS):
            for h in range(2):
                order = first + i if h == 0 else M - 1 - first - i
                exponent = coef_ref[0, 10 * STEPS + h * PAIRS + i] + order.astype(F32) * log_sine
                ramp = jnp.clip((exponent + 75.0) / 10.0, 0.0, 1.0)
                start_ref[h * PAIRS + i] = jnp.exp(jnp.maximum(exponent, -75.0)) * ramp * weight
        for term in range(20):
            code = codes_ref[0, term % 4, term // 4]
            wide_out[term] = jnp.dot(rmap_ref[term], select_ref[code, 0:64, :], preferred_element_type=F32).astype(BF16)
            cols_out[term] = jnp.dot(select_ref[code, 64:192, 0:64], cmap_ref[term], preferred_element_type=F32).astype(BF16)

    cosine = colat_ref[0]

    def advance(base, state, switching):
        state = list(state)
        for k in range(16):
            slot = base + k
            for i in range(PAIRS):
                one, two = state[2 * i], state[2 * i + 1]
                grow = coef_ref[0, (2 * i) * STEPS + slot]
                back = coef_ref[0, (2 * i + 1) * STEPS + slot]
                value = (cosine * grow) * one - two * back
                if switching:
                    value = jnp.where(slot == 0, start_ref[i], value)
                    value = jnp.where(slot == M - first - i, start_ref[PAIRS + i], value)
                state[2 * i], state[2 * i + 1] = value, one
                rows_ref[i, k * 8 : (k + 1) * 8, :] = value
        return tuple(state)

    def sixteen(part, state):
        base = step * CHUNK + part * 16
        switching = (base == 0) | ((base <= M - first) & (base + 16 > M - first - PAIRS))
        state = lax.cond(
            switching, lambda x: advance(base, x, True), lambda x: advance(base, x, False), state
        )
        at = pl.ds(pl.multiple_of(part * 16, 16), 16)
        for i in range(PAIRS):
            for b in range(5):
                value = rows_ref[i, pl.ds(b, 16, stride=8), :]
                high = value.astype(BF16)
                legendre_out[i, at, b * 128 : (b + 1) * 128] = high
                legendre_out[i, at, 640 + b * 128 : 768 + b * 128] = (value - high.astype(F32)).astype(BF16)
        return state

    state = lax.fori_loop(0, CHUNK // 16, sixteen, tuple(state_ref[j] for j in range(2 * PAIRS)))
    for j in range(2 * PAIRS):
        state_ref[j] = state[j]


def sums_kernel(
    first_ref, blocks_ref, table_hbm, out_hbm, table_ref, out_ref, sems, spread_ref, turned_ref, left_ref,
):
    loads = [pltpu.make_async_copy(table_hbm.at[i], table_ref.at[i], sems.at[i]) for i in range(PAIRS)]
    stores = [pltpu.make_async_copy(out_ref.at[i], out_hbm.at[i], sems.at[PAIRS + i]) for i in range(PAIRS)]
    for load in loads:
        load.start()
    lane = lax.broadcasted_iota(jnp.int32, (8, 128), 1)
    for d in range(128):
        spread_ref[d * 16 : (d + 1) * 16, :] = blocks_ref[d].astype(F32)
    for k in range(13):
        parts = [spread_ref[pl.ds(l * 256 + k, 16, stride=16), :] for l in (0, 1, 2, 3, 7, 6, 5, 4)]
        turned_ref[k * 128 : (k + 1) * 128, :] = jnp.concatenate(parts, axis=0).T
    for i in range(PAIRS):
        for h in range(2):
            for b in range(5):
                north, south = [], []
                for c in range(2):
                    base = SLOT[(i, h, c)] * 80 + b * 16
                    one, two = turned_ref[base : base + 8, :], turned_ref[base + 8 : base + 16, :]
                    north.append(jnp.where(lane < 64, one, pltpu.roll(two, 64, 1)))
                    south.append(jnp.where(lane < 64, pltpu.roll(one, 64, 1), two))
                at, again = slice(b * 128, (b + 1) * 128), slice(640 + b * 128, 768 + b * 128)
                north = jnp.concatenate(north, axis=0).astype(BF16)
                left_ref[i, h * 16 : h * 16 + 16, at] = north
                left_ref[i, h * 16 : h * 16 + 16, again] = north
                south = jnp.concatenate(south, axis=0).astype(BF16)
                left_ref[i, 32 + h * 16 : 48 + h * 16, at] = south
                left_ref[i, 32 + h * 16 : 48 + h * 16, again] = south

    slot = lax.broadcasted_iota(jnp.int32, (16, STEPS), 1)
    for i in range(PAIRS):
        loads[i].wait()
        sums = lax.dot_general(left_ref[i], table_ref[i], (((1,), (1,)), ((), ())), preferred_element_type=F32)
        pair = first_ref[0] + i
        low = sums[0:16] + jnp.where(slot & 1 == 0, sums[32:48], -sums[32:48])
        high = sums[16:32] + jnp.where((slot + pair) & 1 == 0, sums[48:64], -sums[48:64])
        result = jnp.where(slot < M - pair, low, high)
        out_ref[i] = result[:, : M + 1]
        stores[i].start()
    for store in stores:
        store.wait()


def vmem(shape=None, index=None):
    if shape is None:
        return pl.BlockSpec(memory_space=pltpu.VMEM)
    return pl.BlockSpec(shape, index)


SMEM = pl.BlockSpec(memory_space=pltpu.SMEM)
HBM = pl.BlockSpec(memory_space=pltpu.HBM)


def params(limit):
    return pltpu.CompilerParams(vmem_limit_bytes=limit * MIB)


def cost(flops, moved):
    return pl.CostEstimate(flops=flops, bytes_accessed=moved, transcendentals=0)


def recurrence_factors():
    pair = np.arange(M // 2)[:, None]
    slot = np.arange(STEPS)[None, :]
    is_low = slot < M - pair
    order = np.where(is_low, pair, M - 1 - pair)
    degree = np.where(is_low, pair + slot, slot - 1)
    grows = (degree > order) & (slot <= M)
    back = (degree - 1 > order) & (slot <= M)
    n2, l2, m2 = degree.astype(np.float64) ** 2, (degree - 1.0) ** 2, order.astype(np.float64) ** 2
    grow = np.where(grows, np.sqrt(np.where(grows, 4 * n2 - 1, 0) / np.where(grows, n2 - m2, 1)), 0)
    keep = np.where(back, grow * np.sqrt(np.where(back, l2 - m2, 0) / np.where(back, 4 * l2 - 1, 1)), 0)
    factors = np.stack([grow, keep], axis=1).reshape(128, 10 * STEPS)
    terms = 0.5 * np.log1p(0.5 / np.arange(1, M, dtype=np.float64))
    logs = np.concatenate([np.zeros(1), np.cumsum(terms)]) + 0.5 * math.log(0.5)
    pair = pair.reshape(128, PAIRS)
    return np.concatenate([factors, logs[pair], logs[M - 1 - pair]], axis=1).astype(np.float32)[:, None]


def selections():
    packed = np.arange(64) % 32 * 2 + np.arange(64) // 32
    rsel, csel = np.zeros((4, 64, 256)), np.zeros((4, 128, 64))
    for code in range(4):
        rows = np.arange(64) if code % 2 else packed
        rows = 63 - rows if code in (1, 2) else rows
        for lev in range(4):
            rsel[code, rows, lev * 64 + np.arange(64)] = 1
        cols = packed if code % 2 else np.arange(64)
        cols = 63 - cols if code in (2, 3) else cols
        csel[code, np.arange(64), cols] = 1
        csel[code, 64 + np.arange(64), cols] = 1
    csel = np.concatenate([csel, np.zeros((4, 128, 192))], axis=2)
    return np.concatenate([rsel, csel], axis=1).astype(BF16)


def legendre_table(device, codes, row_map, col_map):
    colat = latitudes()
    weight = np.pi * np.sin(colat) * math.sqrt(NLAT) / (NLAT + 0.5)
    colat = np.stack([np.cos(colat), np.log(np.sin(colat)), weight]).astype(np.float32)
    table = (PAIRS, STEPS, 1280)
    block = vmem((PAIRS, CHUNK, 1280), lambda g, d: (0, g, 0))
    cols, wide = (20, 128, 160), (20, 32, 256)
    whole = lambda g, d: (0, 0, 0)
    own = pl.BlockSpec((None, 1, 10 * STEPS + 2 * PAIRS), lambda g, d: (d[0], 0, 0), memory_space=pltpu.SMEM)
    return pl.pallas_call(
        table_kernel,
        out_shape=tuple(jax.ShapeDtypeStruct(made, BF16) for made in (table, cols, wide)),
        grid_spec=pltpu.PrefetchScalarGridSpec(
            num_scalar_prefetch=1,
            grid=(STEPS // CHUNK,),
            in_specs=[SMEM, own] + [vmem()] * 4,
            out_specs=(block, vmem(cols, whole), vmem(wide, whole)),
            scratch_shapes=[
                pltpu.VMEM((2 * PAIRS, 8, 128), F32),
                pltpu.VMEM((2 * PAIRS, 8, 128), F32),
                pltpu.VMEM((PAIRS, 128, 128), F32),
            ],
        ),
        compiler_params=params(50),
        cost_estimate=cost(60_000_000, 60_000_000),
        name="legendre_table",
    )(
        device, codes, jnp.asarray(recurrence_factors()), jnp.asarray(colat), row_map, col_map, jnp.asarray(selections()),
    )


def body(source, row_map, col_map, pattern, codes, need_list, owner):
    lat_me = lax.axis_index("lat").astype(jnp.int32)
    tile_me = lax.axis_index("tile").astype(jnp.int32)
    device = tile_me * lax.axis_size("lat") + lat_me
    first = device * PAIRS
    me = lat_me.reshape(1)
    needs = need_list[0]
    outgoing = pl.pallas_call(
        pack_kernel,
        out_shape=jax.ShapeDtypeStruct((8 * MOST, 64, 512), BF16),
        in_specs=[SMEM, SMEM, SMEM, HBM],
        out_specs=HBM,
        scratch_shapes=[
            pltpu.VMEM((7, 8, 4096), BF16),
            pltpu.VMEM((2, 256, 128), F32),
            pltpu.VMEM((7, 64, 512), BF16),
            pltpu.SMEM((8 * MOST + 1,), jnp.int32),
            pltpu.SemaphoreType.DMA((7 + 8 * MOST,)),
        ],
        compiler_params=params(57),
        cost_estimate=cost(1_000_000, 2_000_000),
        name="pack",
    )(owner, needs, me, source)
    incoming = lax.all_to_all(outgoing, "lat", split_axis=0, concat_axis=0, tiled=True)

    code = jnp.transpose(codes, (1, 2, 0))
    table, cols, wide = legendre_table(
        device.reshape(1), code, row_map.reshape(20, 32, 64), col_map.reshape(20, 64, 160)
    )

    field = pl.pallas_call(
        regrid_kernel,
        out_shape=jax.ShapeDtypeStruct((16, 112, 128), BF16),
        in_specs=[SMEM] * 5 + [vmem()] * 3,
        out_specs=vmem(),
        scratch_shapes=[
            pltpu.VMEM((2 * NEED, 512, 128), BF16),
            pltpu.VMEM((2, 256, 128), F32),
            pltpu.VMEM((2, 256, 128), F32),
            pltpu.VMEM((16, 16, 128), F32),
            pltpu.SMEM((8,), jnp.int32),
        ],
        compiler_params=params(14),
        cost_estimate=cost(700_000_000, 5_000_000),
        name="regrid",
    )(owner, needs, me, jnp.transpose(pattern, (1, 2, 0)), code, incoming, cols, wide)
    rows = lax.all_to_all(field, "tile", split_axis=0, concat_axis=0, tiled=True)

    spectral = pl.pallas_call(
        dft_kernel,
        out_shape=jax.ShapeDtypeStruct((128, 16, 128), BF16),
        in_specs=[vmem(), HBM],
        out_specs=vmem(),
        scratch_shapes=[
            pltpu.VMEM((5, 2, 2, 1280, 256), BF16),
            pltpu.SemaphoreType.DMA((5,)),
            pltpu.VMEM((2, 160, 1280), BF16),
            pltpu.VMEM((1664, 128), F32),
            pltpu.VMEM((2048, 128), F32),
        ],
        compiler_params=params(50),
        cost_estimate=cost(1_000_000_000, 14_000_000),
        name="dft",
    )(rows, jnp.asarray(dft_tables()))
    arranged = lax.all_to_all(spectral, ("lat", "tile"), split_axis=0, concat_axis=0, tiled=True)

    return pl.pallas_call(
        sums_kernel,
        out_shape=jax.ShapeDtypeStruct((PAIRS, 2 * LEV, M + 1), F32),
        in_specs=[SMEM, vmem(), HBM],
        out_specs=HBM,
        scratch_shapes=[
            pltpu.VMEM((PAIRS, STEPS, 1280), BF16),
            pltpu.VMEM((PAIRS, 2 * LEV, M + 1), F32),
            pltpu.SemaphoreType.DMA((2 * PAIRS,)),
            pltpu.VMEM((2048, 128), F32),
            pltpu.VMEM((1664, 128), F32),
            pltpu.VMEM((PAIRS, 64, 1280), BF16),
        ],
        compiler_params=params(50),
        cost_estimate=cost(2_000_000_000, 17_000_000),
        name="sums",
    )(first.reshape(1), arranged, table)


def solution(mesh):
    placed = (
        P(("tile", "lat"), None, None),
        P("lat", "tile", None, None, None),
        P("lat", None, None, "tile"),
        P("lat", "tile", None),
        P("lat", "tile", None),
        P("tile", None, None),
        P(),
    )
    return jax.shard_map(
        body, mesh=mesh, in_specs=placed, out_specs=P(("tile", "lat"), None, None), check_vma=False
    )
```
